32 devices in a mesh: seq: 32 (over z, y, x, core), head: 1.
Axes of the slice: x: 2, y: 2, z: 4, core: 2. Of those that a mesh axis runs over, the one named last changes fastest.
Arguments:
- queries: bfloat16 [8192, 4096], P('seq', 'head'), may hold values from -6 to 6
- keys: bfloat16 [8192, 4096], P('seq', 'head'), may hold values from -6 to 6
- values: bfloat16 [8192, 4096], P('seq', 'head'), may hold values from -6 to 6
- gate: bfloat16 [8192, 4096], P('seq', 'head'), may hold values from -6 to 6
- residual: bfloat16 [8192, 4096], P('seq', 'head'), may hold values from -40 to 40
- log_decay: float32 [8192, 32], P('seq', 'head'), may hold values from -1 to 0, as said below
- out_weight: bfloat16 [4096, 4096], P('seq', 'head'), may hold values from -0.09375 to 0.09375
- norm_gain: bfloat16 [4096], P('head'), may hold values from 0.099609375 to 1.8984375
- kv_weight: bfloat16 [4096, 2048], P('seq', 'head'), may hold values from -0.09375 to 0.09375
Outputs:
- cache_keys: bfloat16 [8192, 1024], P('seq', 'head')
- cache_values: bfloat16 [8192, 1024], P('seq', 'head')
The draws below stay inside these ranges and needn't reach their ends.
Inputs may be any that keep to these rules, and one draw needn't show every extreme that they name: `log_decay`: every entry is negative.
All inputs are finite; a program needn't handle non-finite values.
Results may differ from the reference program's by a relative error of at most 0.015.
Values may be sent and summed in bfloat16 or wider, within the bound.
No kernel may reach another device: no remote copies, remote signals or barrier semaphores. Data moves between devices by JAX's collectives and lax.ppermute only.
A program may use at most 192 MiB of HBM per device.

```python
import math
import jax
import jax.numpy as jnp
from jax import lax

H = 32
HD = 128
KV_HEADS = 8
D = 4096
TOK_DEV = 256
LEADING_WORDS = 8192


def draw_log_decay(key, part):
    parts_list = jax.random.split(key, 6)
    share = 0.5
    fast = jax.random.uniform(parts_list[0], (H,)) < share
    fast_rate = 1.0 / 40.0 * jnp.exp(jax.random.uniform(parts_list[1], (H,), minval=-0.35, maxval=0.35))
    slow_rate = 0.5 / LEADING_WORDS * jnp.exp(jax.random.uniform(parts_list[1], (H,), minval=-0.5, maxval=0.4))
    fading_ratio = jnp.where(fast, fast_rate, slow_rate)
    segment_scaling = jnp.exp(jax.random.uniform(parts_list[2], (LEADING_WORDS // TOK_DEV, H), minval=-0.7, maxval=0.7))
    segment_scaling = jnp.repeat(segment_scaling, TOK_DEV, axis=0)
    item_scaling = jnp.exp(jax.random.uniform(parts_list[3], (LEADING_WORDS, H), minval=-0.5, maxval=0.5))
    index_places = jax.random.randint(parts_list[4], (2,), 0, LEADING_WORDS)
    copy_packet = jnp.any(jnp.arange(LEADING_WORDS)[:, None] == index_places[None, :], axis=1).astype(jnp.float32)
    entry_tally = jax.random.uniform(parts_list[5], (LEADING_WORDS, H), minval=0.22, maxval=0.6)
    layer_answer = -(fading_ratio[None, :] * segment_scaling * item_scaling) - copy_packet[:, None] * entry_tally
    return layer_answer.astype(jnp.float32)


def draw_residual(key, part):
    parts_list = jax.random.split(key, 2)
    column = jnp.arange(D, dtype=jnp.float32) / (D - 1)
    colscale = 0.4 * jnp.exp(column * math.log(5.0)) * jax.random.uniform(parts_list[1], (D,), minval=0.7, maxval=1.3)
    base = jnp.clip(jax.random.normal(parts_list[0], (LEADING_WORDS, D)), -6.0, 6.0)
    layer_answer = base * colscale[None, :]
    return layer_answer.astype(jnp.bfloat16)


def steps_of(stream_key, dims, pieces, low, top_value):
    def one(dim, shards_of):
        steps = jax.random.uniform(jax.random.fold_in(jax.random.fold_in(stream_key, 6), dim), (shards_of,), jnp.float32, low / len(pieces), top_value / len(pieces))
        return jnp.repeat(jnp.exp(steps), dims[dim] // shards_of).reshape((-1,) + (1,) * (len(dims) - dim - 1))

    factor_of = one(*pieces[0])
    for cut in pieces[1:]:
        factor_of = factor_of * one(*cut)
    return factor_of


def gaussian(rng, dims, scale, limit, cuts=(), kind=jnp.bfloat16):
    level = steps_of(rng, dims, cuts, -0.22, 0.18) if cuts else 1.0
    values = jax.random.normal(rng, dims, jnp.float32) * scale * level
    return jnp.minimum(jnp.maximum(values, -limit), limit).astype(kind)


def setup_inputs(seed: int = 0) -> dict:
    key_list = jax.random.split(jax.random.key(seed), 10)
    return {
        "queries": gaussian(key_list[0], (LEADING_WORDS, D), 1.0, 6.0, ((0, 32),)),
        "keys": gaussian(key_list[1], (LEADING_WORDS, D), 1.0, 6.0, ((0, 32),)),
        "values": gaussian(key_list[2], (LEADING_WORDS, D), 1.0, 6.0, ((0, 32),)),
        "gate": gaussian(key_list[3], (LEADING_WORDS, D), 1.0, 6.0, ((0, 32),)),
        "residual": draw_residual(jax.random.fold_in(key_list[9], 71), 0),
        "log_decay": draw_log_decay(jax.random.fold_in(key_list[9], 71), 0),
        "out_weight": gaussian(key_list[6], (D, D), D ** -0.5, 0.09375, ((0, 32),)),
        "norm_gain": jnp.clip(1.0 + 0.18 * jax.random.normal(key_list[7], (D,), jnp.float32), 0.099609375, 1.8984375).astype(jnp.bfloat16),
        "kv_weight": gaussian(key_list[8], (D, 2 * KV_HEADS * HD), D ** -0.5, 0.09375, ((0, 32),)),
    }


HIGHEST = lax.Precision.HIGHEST

def local_retention(queries, keys, values, log_decay, block):
    tokens, heads, width = queries.shape
    count = tokens // block

    def to_blocks(array):
        return array.reshape((count, block) + array.shape[1:])
    lower = jnp.arange(block)[:, None] >= jnp.arange(block)[None, :]

    def advance(carry, inputs):
        state, offset = carry
        query_block, key_block, value_block, decay_block = inputs
        within = jnp.cumsum(decay_block, axis=0)
        spread = within[:, None, :] - within[None, :, :]
        factor = jnp.where(lower[:, :, None], jnp.exp(jnp.where(lower[:, :, None], spread, 0.0)), 0.0)
        scores = jnp.einsum('ihd,jhd->hij', query_block.astype(jnp.float32), key_block.astype(jnp.float32), precision=HIGHEST)
        weighted = scores * jnp.transpose(factor, (2, 0, 1))
        values_wide = value_block.astype(jnp.float32)
        intra = jnp.einsum('hij,jhd->ihd', weighted, values_wide, precision=HIGHEST)
        query_wide = query_block.astype(jnp.float32)
        carried = jnp.exp(within)[:, :, None] * jnp.einsum('ihd,hde->ihe', query_wide, state, precision=HIGHEST)
        ending = within[-1]
        key_wide = key_block.astype(jnp.float32) * jnp.exp(ending[None, :] - within)[:, :, None]
        fresh = jnp.exp(ending)[:, None, None] * state + jnp.einsum('jhd,jhe->hde', key_wide, values_wide, precision=HIGHEST)
        return ((fresh, offset + ending), (intra + carried, offset[None, :] + within))
    start = (jnp.zeros((heads, width, width), jnp.float32), jnp.zeros((heads,), jnp.float32))
    final, stacked = lax.scan(advance, start, (to_blocks(queries), to_blocks(keys), to_blocks(values), to_blocks(log_decay)))
    return (stacked[0].reshape(tokens, heads, width), stacked[1].reshape(tokens, heads), final[0], final[1])

def reference(queries, keys, values, gate, residual, log_decay, out_weight, norm_gain, kv_weight):
    shaped = [array.reshape(LEADING_WORDS, H, HD) for array in (queries, keys, values)]
    retained, running, state, offset = local_retention(shaped[0], shaped[1], shaped[2], log_decay, min(512, LEADING_WORDS))
    scale = lax.rsqrt(lax.optimization_barrier(jnp.mean(retained * retained, axis=2, keepdims=True)) + 1e-06)
    mixed = (jax.nn.silu(gate.astype(jnp.float32)) * (retained * scale).reshape(LEADING_WORDS, D)).astype(jnp.bfloat16)
    branch = jnp.dot(mixed, out_weight, preferred_element_type=jnp.float32)
    hidden = (residual.astype(jnp.float32) + branch).astype(jnp.bfloat16)
    wide = hidden.astype(jnp.float32)
    inverse = lax.rsqrt(lax.optimization_barrier(jnp.mean(wide * wide, axis=1, keepdims=True)) + 1e-06)
    normalized = (wide * inverse * norm_gain.astype(jnp.float32)[None, :]).astype(jnp.bfloat16)
    projected = jnp.dot(normalized, kv_weight, preferred_element_type=jnp.float32).reshape(LEADING_WORDS, KV_HEADS, 2, HD)
    cache_keys = projected[:, :, 0, :].reshape(LEADING_WORDS, KV_HEADS * HD).astype(jnp.bfloat16)
    cache_values = projected[:, :, 1, :].reshape(LEADING_WORDS, KV_HEADS * HD).astype(jnp.bfloat16)
    return (cache_keys, cache_values)
```

```python
import functools
import math

import jax
import jax.numpy as jnp
from jax import lax
from jax.experimental import pallas as pl
from jax.experimental.pallas import tpu as pltpu
from jax.sharding import Mesh
from jax.sharding import PartitionSpec as P

F32, BF16 = jnp.float32, jnp.bfloat16
HIGHEST = lax.Precision.HIGHEST
NORM_EPS = 1e-06
DECAY_ROWS = 16
FAR = ("z", "y")
PLANE = ("y", "x", "c")
SEQ = ("z", "y", "x", "c")
VMEM_LIMIT = 48 * 1024 * 1024


def params():
    return pltpu.CompilerParams(vmem_limit_bytes=VMEM_LIMIT)


def split_rows(total):
    high = total.astype(BF16).astype(F32)
    middle = (total - high).astype(BF16).astype(F32)
    low = total - high - middle
    row = lax.broadcasted_iota(jnp.int32, (DECAY_ROWS, total.shape[1]), 0)
    rows = jnp.where(row == 0, high, jnp.where(row == 1, middle, jnp.where(row == 2, low, 0.0)))
    return rows.astype(BF16)


def join_rows(rows):
    return jnp.sum(rows.astype(F32), axis=0, keepdims=True)


def dot(a, b, contract):
    return lax.dot_general(a, b, (contract, ((), ())), preferred_element_type=F32)


def state_kernel(width, key_ref, value_ref, within_ref, state_ref):
    tokens = key_ref.shape[0]
    within = within_ref[0]
    ending = within[tokens - 1 : tokens, :]
    fade = jnp.exp(ending - within)
    for head in range(state_ref.shape[0]):
        columns = slice(head * width, (head + 1) * width)
        faded = (key_ref[:, columns].astype(F32) * fade[:, head : head + 1]).astype(BF16)
        state = dot(faded, value_ref[:, columns], ((0,), (0,)))
        state_ref[head, :width, :] = state.astype(BF16)
        total = jnp.broadcast_to(ending[:, head : head + 1], (1, width))
        state_ref[head, width:, :] = split_rows(total)


def intra_kernel(width, query_ref, key_ref, value_ref, within_ref, across_ref, out_ref):
    tokens = query_ref.shape[0]
    within, across = within_ref[0], across_ref[0]
    lower = lax.broadcasted_iota(jnp.int32, (tokens, tokens), 0) >= lax.broadcasted_iota(
        jnp.int32, (tokens, tokens), 1
    )
    for head in range(within.shape[1]):
        columns = slice(head * width, (head + 1) * width)
        scores = dot(query_ref[:, columns], key_ref[:, columns], ((1,), (1,)))
        spread = within[:, head : head + 1] - across[head : head + 1, :]
        weighted = jnp.where(lower, scores * jnp.exp(jnp.where(lower, spread, 0.0)), 0.0)
        out_ref[:, columns] = dot(weighted.astype(BF16), value_ref[:, columns], ((1,), (0,)))


def mix_kernel(width, query_ref, gate_ref, intra_ref, within_ref, state_ref, out_ref):
    reach = jnp.exp(within_ref[0])
    for head in range(state_ref.shape[0]):
        columns = slice(head * width, (head + 1) * width)
        carried = dot(query_ref[:, columns], state_ref[head], ((1,), (0,)))
        retained = intra_ref[:, columns] + reach[:, head : head + 1] * carried
        scale = lax.rsqrt(jnp.mean(retained * retained, axis=1, keepdims=True) + NORM_EPS)
        gate = gate_ref[:, columns].astype(F32)
        out_ref[:, columns] = (gate / (1.0 + jnp.exp(-gate)) * (retained * scale)).astype(BF16)


def total_kernel(width, parts_ref, out_ref):
    state = jnp.zeros((width, width), F32)
    total = jnp.zeros((1, width), F32)
    for place in range(parts_ref.shape[0]):
        ending = join_rows(parts_ref[place, 0, width:, :])
        state = jnp.exp(ending) * state + parts_ref[place, 0, :width, :].astype(F32)
        total = total + ending
    out_ref[0, :width, :] = state.astype(BF16)
    out_ref[0, width:, :] = split_rows(total)


def prefix_kernel(width, planes, parts_ref, *refs):
    plane_refs, out_ref = refs[:planes], refs[planes]
    state = jnp.zeros((width, width), F32)
    reach = jnp.zeros((1, width), F32)
    for ref in plane_refs:
        state = state + jnp.exp(reach) * ref[0, :width, :].astype(F32)
        reach = reach + join_rows(ref[0, width:, :])
    for place in range(parts_ref.shape[0]):
        out_ref[place, 0] = state.astype(BF16)
        ending = join_rows(parts_ref[place, 0, width:, :])
        state = jnp.exp(ending) * state + parts_ref[place, 0, :width, :].astype(F32)


def head_blocks(tokens, columns):
    return pl.BlockSpec((tokens, columns), lambda i: (0, i))


def group_blocks(shape):
    return pl.BlockSpec((1,) + shape, lambda i: (i, 0, 0))


def local_states(keys, values, within, width):
    tokens, groups, per = keys.shape[0], within.shape[0], within.shape[2]
    wide = head_blocks(tokens, per * width)
    rows = width + DECAY_ROWS
    return pl.pallas_call(
        functools.partial(state_kernel, width),
        grid=(groups,),
        in_specs=[wide, wide, group_blocks((tokens, per))],
        out_specs=pl.BlockSpec((per, rows, width), lambda i: (i, 0, 0)),
        out_shape=jax.ShapeDtypeStruct((groups * per, rows, width), BF16),
        compiler_params=params(),
        name="local_states",
    )(keys, values, within)


def local_intra(queries, keys, values, within, across, width):
    tokens, groups, per = keys.shape[0], within.shape[0], within.shape[2]
    wide = head_blocks(tokens, per * width)
    return pl.pallas_call(
        functools.partial(intra_kernel, width),
        grid=(groups,),
        in_specs=[wide, wide, wide, group_blocks((tokens, per)), group_blocks((per, tokens))],
        out_specs=wide,
        out_shape=jax.ShapeDtypeStruct(queries.shape, F32),
        compiler_params=params(),
        name="local_intra",
    )(queries, keys, values, within, across)


def mix(queries, gate, intra, within, states, width):
    tokens, groups, per = queries.shape[0], within.shape[0], within.shape[2]
    wide = head_blocks(tokens, per * width)
    return pl.pallas_call(
        functools.partial(mix_kernel, width),
        grid=(groups,),
        in_specs=[
            wide,
            wide,
            wide,
            group_blocks((tokens, per)),
            pl.BlockSpec((per, width, width), lambda i: (i, 0, 0)),
        ],
        out_specs=wide,
        out_shape=jax.ShapeDtypeStruct(queries.shape, BF16),
        compiler_params=params(),
        name="mix",
    )(queries, gate, intra, within, states)


def plane_total(parts, width):
    places, heads, rows, _ = parts.shape
    return pl.pallas_call(
        functools.partial(total_kernel, width),
        grid=(heads,),
        in_specs=[pl.BlockSpec((places, 1, rows, width), lambda i: (0, i, 0, 0))],
        out_specs=pl.BlockSpec((1, rows, width), lambda i: (i, 0, 0)),
        out_shape=jax.ShapeDtypeStruct((heads, rows, width), BF16),
        compiler_params=params(),
        name="plane_total",
    )(parts)


def plane_prefix(parts, planes, width):
    places, heads, rows, _ = parts.shape
    return pl.pallas_call(
        functools.partial(prefix_kernel, width, len(planes)),
        grid=(heads,),
        in_specs=[pl.BlockSpec((places, 1, rows, width), lambda i: (0, i, 0, 0))]
        + [pl.BlockSpec((1, rows, width), lambda i: (i, 0, 0))] * len(planes),
        out_specs=pl.BlockSpec((places, 1, width, width), lambda i: (0, i, 0, 0)),
        out_shape=jax.ShapeDtypeStruct((places, heads, width, width), BF16),
        compiler_params=params(),
        name="plane_prefix",
    )(parts, *planes)


def swap(array, devices, distance):
    return lax.ppermute(array, SEQ, [(i, i ^ distance) for i in range(devices)])


def pick(array, index, axis):
    return lax.dynamic_index_in_dim(array, index, axis, keepdims=False)


def shared_on_device(
    sizes, queries, keys, values, gate, residual, log_decay, out_weight, norm_gain, kv_weight
):
    depth, near = sizes[0], sizes[2] * sizes[3]
    devices = math.prod(sizes)
    far, places = sizes[0] * sizes[1], sizes[1] * near
    tokens, heads = log_decay.shape
    width = queries.shape[1] // heads
    model = out_weight.shape[1]
    rows = out_weight.shape[0]
    cache = kv_weight.shape[1] // 2
    core, side = lax.axis_index("c"), lax.axis_index("x")
    here = 2 * side + core

    def columns_of(array, place):
        shaped = array.reshape(array.shape[0], far, near, model // (far * near))
        return pick(shaped, place, 2).reshape(array.shape[0], model // near)

    with jax.named_scope("out_weight_gather"):
        shard = jnp.zeros((near, rows, model // near), BF16)
        for other in range(near):
            piece = columns_of(out_weight, here ^ other)
            if other:
                piece = swap(piece, devices, other)
            shard = lax.dynamic_update_index_in_dim(shard, piece, here ^ other, 0)
        out_full = lax.all_gather(
            shard.reshape(near * rows, model // near), FAR, axis=0, tiled=True
        )
    with jax.named_scope("kv_weight_gather"):
        shaped = kv_weight.reshape(rows, cache // width, 2, width)
        mine = pick(shaped, core, 2).reshape(rows, cache)
        other = swap(pick(shaped, 1 - core, 2).reshape(rows, cache), devices, 1)
        kv_full = lax.all_gather(jnp.stack([mine, other]), FAR, axis=0)
        kv_mine = kv_full[:, 0].reshape(far * rows, cache)
        kv_other = kv_full[:, 1].reshape(far * rows, cache)

    with jax.named_scope("residual_exchange"):
        residuals = [columns_of(residual, here)]
        for other in range(1, near):
            residuals.append(swap(columns_of(residual, here ^ other), devices, other))

    per = heads // places
    running = jnp.cumsum(log_decay, axis=0)
    within = running.reshape(tokens, places, per).transpose(1, 0, 2)
    across = running.T.reshape(places, per, tokens)
    with jax.named_scope("state_scan"):
        states = local_states(keys, values, within, width)
        states = states.reshape((places, per) + states.shape[1:])
        parts = lax.all_to_all(states, PLANE, 0, 0, tiled=True)
        total = plane_total(parts, width)
        step = devices // depth
        planes = [
            lax.ppermute(total, SEQ, [(i, i + d * step) for i in range(devices - d * step)])
            for d in range(1, depth)
        ]
        entering = lax.all_to_all(plane_prefix(parts, planes, width), PLANE, 0, 0, tiled=True)
        entering = entering.reshape(heads, width, width)
    intra = local_intra(queries, keys, values, within, across, width)
    mixed = mix(queries, gate, intra, within, entering, width)

    with jax.named_scope("mixed_exchange"):
        mixes = [mixed, swap(mixed, devices, 1), swap(mixed, devices, 2)]
        mixes.append(swap(mixes[2], devices, 1))

    with jax.named_scope("out_projection"):
        gain = pick(norm_gain.reshape(far, near, model // (far * near)), here, 1)
        gain = gain.reshape(1, model // near).astype(F32)
        squares, scaled = [], []
        for block, start in zip(mixes, residuals):
            branch = jnp.dot(block, out_full, preferred_element_type=F32)
            hidden = (start.astype(F32) + branch).astype(BF16).astype(F32)
            squares.append(jnp.sum(hidden * hidden, axis=1))
            scaled.append((hidden * gain).astype(BF16))
        squares = jnp.stack(squares)
        squares = squares + swap(squares, devices, 1)[jnp.array([1, 0, 3, 2])]
        squares = squares[:2] + swap(squares[2:], devices, 2)
        inverse = lax.rsqrt(squares / model + NORM_EPS)

    with jax.named_scope("cache_projection"):

        def partial(block, received):
            return jnp.dot(block, kv_mine, preferred_element_type=F32) + jnp.dot(
                received, kv_other, preferred_element_type=F32
            )

        received = swap(jnp.stack([scaled[3], scaled[2], scaled[1], scaled[0]]), devices, 1)
        away = [
            partial(scaled[2], received[0]).astype(BF16),
            partial(scaled[3], received[1]).astype(BF16),
        ]
        back = swap(jnp.stack(away), devices, 2)
        home = [partial(scaled[0], received[2]), partial(scaled[1], received[3])]
        done = [
            ((home[i] + back[i].astype(F32)) * inverse[i][:, None]).astype(BF16) for i in range(2)
        ]
        swapped = swap(done[1], devices, 1)
        first = core == 0
        return (jnp.where(first, done[0], swapped), jnp.where(first, swapped, done[0]))


def entering(part, axis, combine, identity):
    place = lax.axis_index(axis)
    gathered = jax.tree.map(lambda a: lax.all_gather(a, axis), part)
    state = jax.tree.map(lambda a, e: jnp.zeros_like(a) + jnp.asarray(e, a.dtype), part, identity)

    def one(step, state):
        return combine(
            state, jax.tree.map(lambda a: lax.dynamic_index_in_dim(a, step, 0, False), gathered)
        )

    return lax.fori_loop(0, place, one, state)


def local_retention(queries, keys, values, log_decay, block):
    tokens, heads, width = queries.shape
    count = tokens // block

    def to_blocks(array):
        return array.reshape((count, block) + array.shape[1:])

    lower = jnp.arange(block)[:, None] >= jnp.arange(block)[None, :]

    def advance(carry, inputs):
        state, offset = carry
        query_block, key_block, value_block, decay_block = inputs
        within = jnp.cumsum(decay_block, axis=0)
        spread = within[:, None, :] - within[None, :, :]
        factor = jnp.where(
            lower[:, :, None], jnp.exp(jnp.where(lower[:, :, None], spread, 0.0)), 0.0
        )
        scores = jnp.einsum(
            "ihd,jhd->hij", query_block, key_block, preferred_element_type=jnp.float32
        )
        weighted = scores * jnp.transpose(factor, (2, 0, 1))
        values_wide = value_block.astype(jnp.float32)
        intra = jnp.einsum("hij,jhd->ihd", weighted, values_wide, precision=HIGHEST)
        query_wide = query_block.astype(jnp.float32)
        carried = jnp.exp(within)[:, :, None] * jnp.einsum(
            "ihd,hde->ihe", query_wide, state, precision=HIGHEST
        )
        ending = within[-1]
        key_wide = key_block.astype(jnp.float32) * jnp.exp(ending[None, :] - within)[:, :, None]
        fresh = jnp.exp(ending)[:, None, None] * state + jnp.einsum(
            "jhd,jhe->hde", key_wide, values_wide, precision=HIGHEST
        )
        return ((fresh, offset + ending), (intra + carried, offset[None, :] + within))

    start = (jnp.zeros((heads, width, width), jnp.float32), jnp.zeros((heads,), jnp.float32))
    final, stacked = lax.scan(
        advance,
        start,
        (to_blocks(queries), to_blocks(keys), to_blocks(values), to_blocks(log_decay)),
    )
    return (
        stacked[0].reshape(tokens, heads, width),
        stacked[1].reshape(tokens, heads),
        final[0],
        final[1],
    )


def combine_states(earlier, later):
    return (earlier[0] * later[0], later[0][:, None, None] * earlier[1] + later[1])


def on_device(queries, keys, values, gate, residual, log_decay, out_weight, norm_gain, kv_weight):
    tokens = queries.shape[0]
    heads = log_decay.shape[1]
    width = queries.shape[1] // heads
    shaped = [array.reshape(tokens, heads, width) for array in (queries, keys, values)]
    partial_out, running, state, offset = local_retention(
        shaped[0], shaped[1], shaped[2], log_decay, min(512, tokens)
    )
    identity = (jnp.ones((heads,), jnp.float32), jnp.zeros((heads, width, width), jnp.float32))
    scan_decay, incoming = entering((jnp.exp(offset), state), "seq", combine_states, identity)
    retained = partial_out + jnp.exp(running)[:, :, None] * jnp.einsum(
        "thd,hde->the", shaped[0].astype(jnp.float32), incoming, precision=HIGHEST
    )
    scale = lax.rsqrt(jnp.mean(retained * retained, axis=2, keepdims=True) + 1e-06)
    mixed = (
        jax.nn.silu(gate.astype(jnp.float32)) * (retained * scale).reshape(tokens, heads * width)
    ).astype(jnp.bfloat16)
    all_heads = lax.all_gather(mixed, "head", axis=1, tiled=True)
    out_full, kv_full = (
        lax.all_gather(out_weight, "seq", axis=0, tiled=True),
        lax.all_gather(kv_weight, "seq", axis=0, tiled=True),
    )
    branch = jnp.dot(all_heads, out_full, preferred_element_type=jnp.float32)
    hidden = (residual.astype(jnp.float32) + branch).astype(jnp.bfloat16)
    wide = hidden.astype(jnp.float32)
    squares = lax.psum(jnp.sum(wide * wide, axis=1), "head")
    features = wide.shape[1] * lax.axis_size("head")
    inverse = lax.rsqrt(squares[:, None] / features + 1e-06)
    local_norm = (wide * inverse * norm_gain.astype(jnp.float32)[None, :]).astype(jnp.bfloat16)
    normalized = lax.all_gather(local_norm, "head", axis=1, tiled=True)
    projected = jnp.dot(normalized, kv_full, preferred_element_type=jnp.float32)
    cache_heads = kv_weight.shape[1] // (2 * width)
    arranged = projected.reshape(tokens, cache_heads, 2, width)
    cache_keys = arranged[:, :, 0, :].reshape(tokens, cache_heads * width).astype(jnp.bfloat16)
    cache_values = arranged[:, :, 1, :].reshape(tokens, cache_heads * width).astype(jnp.bfloat16)
    return (cache_keys, cache_values)


def sequence_sizes(devices):
    return (devices // 8, 2, 2, 2)


def solution(mesh):
    devices, split = mesh.shape["seq"], mesh.shape["head"]
    if split == 1 and devices % 8 == 0:
        sizes = sequence_sizes(devices)
        fine = Mesh(mesh.devices.reshape(sizes + (1,)), SEQ + ("head",))
        tokens, copied = P(SEQ, "head"), P("head")
        return jax.shard_map(
            functools.partial(shared_on_device, sizes),
            mesh=fine,
            in_specs=(tokens,) * 7 + (copied, tokens),
            out_specs=(tokens, tokens),
            check_vma=False,
        )
    placed = (P("seq", "head"),) * 7 + (P("head"), P("seq", "head"))
    return jax.shard_map(
        on_device,
        mesh=mesh,
        in_specs=placed,
        out_specs=(P("seq", "head"), P("seq", "head")),
        check_vma=False,
    )
```

```python
import functools
import math

import jax
import jax.numpy as jnp
from jax import lax
from jax.experimental import pallas as pl
from jax.experimental.pallas import tpu as pltpu
from jax.sharding import Mesh
from jax.sharding import PartitionSpec as P

F32, BF16 = jnp.float32, jnp.bfloat16
HIGHEST = lax.Precision.HIGHEST
NORM_EPS = 1e-06
DECAY_ROWS = 16
PLANE = ("y", "x", "c")
SEQ = ("z", "y", "x", "c")
VMEM_LIMIT = 16 * 1024 * 1024


def split_rows(total):
    high = total.astype(BF16).astype(F32)
    middle = (total - high).astype(BF16).astype(F32)
    low = total - high - middle
    row = lax.broadcasted_iota(jnp.int32, (DECAY_ROWS, total.shape[1]), 0)
    rows = jnp.where(row == 0, high, jnp.where(row == 1, middle, jnp.where(row == 2, low, 0.0)))
    return rows.astype(BF16)


def join_rows(rows):
    return jnp.sum(rows.astype(F32), axis=0, keepdims=True)


def dot(a, b, contract):
    return lax.dot_general(a, b, (contract, ((), ())), preferred_element_type=F32)


def state_kernel(width, key_ref, value_ref, within_ref, out_ref):
    tokens = key_ref.shape[0]
    within = within_ref[0]
    ending = within[tokens - 1 : tokens, :]
    fade = jnp.exp(ending - within)
    rows = width + DECAY_ROWS
    for head in range(within.shape[1]):
        columns = slice(head * width, (head + 1) * width)
        faded = (key_ref[:, columns].astype(F32) * fade[:, head : head + 1]).astype(BF16)
        state = dot(faded, value_ref[:, columns], ((0,), (0,)))
        out_ref[0, head * rows : head * rows + width, :] = state.astype(BF16)
        total = jnp.broadcast_to(ending[:, head : head + 1], (1, width))
        out_ref[0, head * rows + width : (head + 1) * rows, :] = split_rows(total)


def intra_kernel(
    width, query_ref, key_ref, value_ref, gate_ref, within_ref, across_ref, out_ref, open_ref
):
    tokens = query_ref.shape[0]
    within, across = within_ref[0], across_ref[0]
    lower = lax.broadcasted_iota(jnp.int32, (tokens, tokens), 0) >= lax.broadcasted_iota(
        jnp.int32, (tokens, tokens), 1
    )
    for head in range(within.shape[1]):
        columns = slice(head * width, (head + 1) * width)
        scores = dot(query_ref[:, columns], key_ref[:, columns], ((1,), (1,)))
        spread = within[:, head : head + 1] - across[head : head + 1, :]
        weighted = jnp.where(lower, scores * jnp.exp(jnp.where(lower, spread, 0.0)), 0.0)
        out_ref[:, columns] = dot(weighted.astype(BF16), value_ref[:, columns], ((1,), (0,)))
        gate = gate_ref[:, columns].astype(F32)
        open_ref[:, columns] = (gate / (1.0 + jnp.exp(-gate))).astype(BF16)


def mix_kernel(width, query_ref, open_ref, intra_ref, within_ref, state_ref, *out_refs):
    reach = jnp.exp(within_ref[0])
    rows = out_refs[0].shape[0]
    for head in range(state_ref.shape[0]):
        columns = slice(head * width, (head + 1) * width)
        carried = dot(query_ref[:, columns], state_ref[head], ((1,), (0,)))
        retained = intra_ref[:, columns] + reach[:, head : head + 1] * carried
        scale = lax.rsqrt(jnp.mean(retained * retained, axis=1, keepdims=True) + NORM_EPS)
        mixed = (open_ref[:, columns].astype(F32) * (retained * scale)).astype(BF16)
        for half, out_ref in enumerate(out_refs):
            out_ref[:, columns] = mixed[half * rows : (half + 1) * rows]


def total_kernel(width, parts_ref, out_ref):
    state = jnp.zeros((width, width), F32)
    total = jnp.zeros((1, width), F32)
    for place in range(parts_ref.shape[0]):
        ending = join_rows(parts_ref[place, width:, :])
        state = jnp.exp(ending) * state + parts_ref[place, :width, :].astype(F32)
        total = total + ending
    out_ref[0, :width, :] = state.astype(BF16)
    out_ref[0, width:, :] = split_rows(total)


def prefix_kernel(width, planes, parts_ref, *refs):
    plane_refs, out_ref = refs[:planes], refs[planes]
    state = jnp.zeros((width, width), F32)
    reach = jnp.zeros((1, width), F32)
    for ref in plane_refs:
        state = state + jnp.exp(reach) * ref[0, :width, :].astype(F32)
        reach = reach + join_rows(ref[0, width:, :])
    for place in range(parts_ref.shape[0]):
        out_ref[place, 0] = state.astype(BF16)
        ending = join_rows(parts_ref[place, width:, :])
        state = jnp.exp(ending) * state + parts_ref[place, :width, :].astype(F32)


def local_call(
    name, body, grid, operands, specs, out_specs, out_shape, scalars=(), scratch=(), after=()
):
    taken = len(scalars) + len(operands)

    def kernel(*refs):
        body(*refs[:taken], *refs[taken + len(after) :])

    return pl.pallas_call(
        kernel,
        grid_spec=pltpu.PrefetchScalarGridSpec(
            num_scalar_prefetch=len(scalars),
            grid=(grid,),
            in_specs=list(specs) + [pl.BlockSpec(memory_space=pltpu.HBM)] * len(after),
            out_specs=out_specs,
            scratch_shapes=scratch,
        ),
        out_shape=out_shape,
        compiler_params=pltpu.CompilerParams(vmem_limit_bytes=VMEM_LIMIT),
        name=name,
    )(*scalars, *operands, *after)


def wide(rows, columns):
    return pl.BlockSpec((rows, columns), lambda i, *_: (0, i))


def whole(rows, columns):
    return pl.BlockSpec((rows, columns), lambda i, *_: (0, 0))


def group(*shape):
    return pl.BlockSpec((1,) + shape, lambda i, *_: (i, 0, 0))


def local_states(keys, values, within, width, after=()):
    tokens, groups, per = keys.shape[0], within.shape[0], within.shape[2]
    tall = per * (width + DECAY_ROWS)
    return local_call(
        "local_states",
        functools.partial(state_kernel, width),
        groups,
        (keys, values, within),
        (wide(tokens, per * width), wide(tokens, per * width), group(tokens, per)),
        group(tall, width),
        jax.ShapeDtypeStruct((groups, tall, width), BF16),
        after=after,
    )


def local_intra(queries, keys, values, gate, within, across, width, after=()):
    tokens, groups, per = keys.shape[0], within.shape[0], within.shape[2]
    heads = wide(tokens, per * width)
    return local_call(
        "local_intra",
        functools.partial(intra_kernel, width),
        groups,
        (queries, keys, values, gate, within, across),
        (heads, heads, heads, heads, group(tokens, per), group(per, tokens)),
        [heads, heads],
        [
            jax.ShapeDtypeStruct(queries.shape, F32),
            jax.ShapeDtypeStruct(queries.shape, BF16),
        ],
        after=after,
    )


def mix(queries, opened, intra, within, states, width, after=()):
    groups, tokens, per = within.shape
    heads = wide(tokens, per * width)
    return local_call(
        "mix",
        functools.partial(mix_kernel, width),
        groups,
        (queries, opened, intra, within, states),
        (
            heads,
            heads,
            heads,
            group(tokens, per),
            pl.BlockSpec((per, width, width), lambda i: (i, 0, 0)),
        ),
        [wide(tokens // 2, per * width)] * 2,
        [jax.ShapeDtypeStruct((tokens // 2, queries.shape[1]), BF16)] * 2,
        after=after,
    )


def plane_total(parts, heads, width, after=()):
    places, rows = parts.shape[0], width + DECAY_ROWS
    return local_call(
        "plane_total",
        functools.partial(total_kernel, width),
        heads,
        (parts,),
        (pl.BlockSpec((places, rows, width), lambda i: (0, i, 0)),),
        group(rows, width),
        jax.ShapeDtypeStruct((heads, rows, width), BF16),
        after=after,
    )


def plane_prefix(parts, planes, width, after=()):
    places, (heads, rows, _) = parts.shape[0], planes[0].shape
    return local_call(
        "plane_prefix",
        functools.partial(prefix_kernel, width, len(planes)),
        heads,
        (parts, *planes),
        [pl.BlockSpec((places, rows, width), lambda i: (0, i, 0))]
        + [group(rows, width)] * len(planes),
        pl.BlockSpec((places, 1, width, width), lambda i: (0, i, 0, 0)),
        jax.ShapeDtypeStruct((places, heads, width, width), BF16),
        after=after,
    )


def deal_kernel(ways, block, place_ref, source_ref, *target_refs):
    for r, target_ref in enumerate(target_refs):
        for i in range(target_ref.shape[1] // block):
            start = pl.multiple_of((i * ways + (place_ref[0] ^ r)) * block, block)
            target_ref[:, i * block : (i + 1) * block] = source_ref[:, pl.ds(start, block)]


def deal(array, place, ways, block, after=()):
    rows, columns = array.shape
    return local_call(
        "deal",
        functools.partial(deal_kernel, ways, block),
        1,
        (array,),
        (whole(rows, columns),),
        [whole(rows, columns // ways)] * ways,
        [jax.ShapeDtypeStruct((rows, columns // ways), array.dtype)] * ways,
        scalars=(place.reshape(1),),
        after=after,
    )


def spread_kernel(block, source_ref, target_ref):
    ways, _, columns = target_ref.shape
    for place in range(ways):
        for i in range(columns // block):
            start = (i * ways + place) * block
            target_ref[place, :, i * block : (i + 1) * block] = source_ref[:, start : start + block]


def spread(array, ways, block, after=()):
    rows, columns = array.shape
    return local_call(
        "spread",
        functools.partial(spread_kernel, block),
        2,
        (array,),
        (pl.BlockSpec((rows // 2, columns), lambda i: (i, 0)),),
        pl.BlockSpec((ways, rows // 2, columns // ways), lambda i: (0, i, 0)),
        jax.ShapeDtypeStruct((ways, rows, columns // ways), array.dtype),
        after=after,
    )


def order_kernel(place_ref, *refs):
    *sources, target_ref = refs
    rows = sources[0].shape[0]
    for r, source in enumerate(sources):
        start = pl.multiple_of((place_ref[0] ^ r) * rows, rows)
        target_ref[pl.ds(start, rows), :] = source[...]


def in_order(arrays, place, after=()):
    rows, columns = arrays[0].shape
    tall = (len(arrays) * rows, columns)
    return local_call(
        "in_order",
        order_kernel,
        1,
        arrays,
        [whole(rows, columns)] * len(arrays),
        whole(*tall),
        jax.ShapeDtypeStruct(tall, arrays[0].dtype),
        scalars=(place.reshape(1),),
        after=after,
    )


def hold(array, after):
    kept = pl.BlockSpec(memory_space=pltpu.HBM)
    return pl.pallas_call(
        lambda *refs: None,
        in_specs=[kept] * (1 + len(after)),
        out_specs=kept,
        out_shape=jax.ShapeDtypeStruct(array.shape, array.dtype),
        input_output_aliases={0: 0},
        compiler_params=pltpu.CompilerParams(vmem_limit_bytes=VMEM_LIMIT),
        name="hold",
    )(array, *after)


def resident(count):
    return [pl.BlockSpec(memory_space=pltpu.VMEM)] * count


def out_kernel(chips, halves, place_ref, *refs):
    pieces = 2 * len(chips)
    mixed, (weight_ref, start_ref, mine_ref, theirs_ref) = refs[:pieces], refs[pieces:]
    tokens, depth = mixed[0].shape
    step = min(depth, 512)
    total = jnp.zeros((pieces * tokens, weight_ref.shape[1]), F32)
    for start in range(0, depth, step):
        left = jnp.concatenate([ref[:, start : start + step] for ref in mixed], axis=0)
        total = total + dot(left, weight_ref[start : start + step, :], ((1,), (0,)))
    for i in range(pieces):
        rows = ((place_ref[0] ^ (2 * chips[i // 2] + i % 2)) * 2 + halves[i // 2]) * tokens
        hidden = start_ref[pl.ds(pl.multiple_of(rows, tokens), tokens), :].astype(F32)
        hidden = (hidden + total[i * tokens : (i + 1) * tokens]).astype(BF16)
        (mine_ref, theirs_ref)[i % 2][i // 2 * tokens : (i // 2 + 1) * tokens, :] = hidden


def out_projection(place, pieces, weight, start, after=()):
    chips, halves, mixed = zip(*pieces)
    mixed = [array for cores in mixed for array in cores]
    shape = jax.ShapeDtypeStruct((len(pieces) * mixed[0].shape[0], weight.shape[1]), BF16)
    return resident_call(
        "out_projection",
        functools.partial(out_kernel, chips, halves),
        (place.reshape(1),),
        (*mixed, weight, start),
        [shape, shape],
        after,
    )


def resident_call(name, body, scalars, operands, out_shape, after):
    taken = len(scalars) + len(operands)

    def kernel(*refs):
        body(*refs[:taken], *refs[taken + len(after) :])

    return pl.pallas_call(
        kernel,
        in_specs=[pl.BlockSpec(memory_space=pltpu.SMEM)] * len(scalars)
        + resident(len(operands))
        + [pl.BlockSpec(memory_space=pltpu.HBM)] * len(after),
        out_specs=resident(len(out_shape)),
        out_shape=out_shape,
        compiler_params=pltpu.CompilerParams(vmem_limit_bytes=VMEM_LIMIT),
        name=name,
    )(*scalars, *operands, *after)


def cache_kernel(width, model, joined, finish, *refs):
    own_ref, other_ref, own_weight_ref, other_weight_ref, *refs = refs
    added, out_refs = refs[: len(joined)], refs[len(joined) :]
    tokens, columns = own_ref.shape[0] // 2, own_weight_ref.shape[1]
    own, other = own_ref[...], other_ref[...]
    total = dot(own, own_weight_ref[...], ((1,), (0,)))
    total = total + dot(other, other_weight_ref[...], ((1,), (0,)))
    squares = jnp.square(own.astype(F32)) + jnp.square(other.astype(F32))
    squares = jnp.sum(squares, axis=1, keepdims=True)
    for i in range(2):
        rows = slice(i * tokens, (i + 1) * tokens)
        sums, norm = total[rows], squares[rows]
        for ref, half in zip(added, joined):
            if half == i:
                sums = sums + ref[:, :columns].astype(F32)
                norm = norm + jnp.sum(ref[:, columns:].astype(F32), axis=1, keepdims=True)
        if finish:
            sums = (sums * lax.rsqrt(norm / model + NORM_EPS)).astype(BF16)
            for head in range(columns // (2 * width)):
                for kind, out_ref in enumerate(out_refs):
                    start = (2 * head + kind) * width
                    out_ref[rows, head * width : (head + 1) * width] = sums[:, start : start + width]
        else:
            high = norm.astype(BF16).astype(F32)
            middle = (norm - high).astype(BF16).astype(F32)
            low = norm - high - middle
            lane = lax.broadcasted_iota(jnp.int32, (tokens, width), 1)
            lanes = jnp.where(lane == 0, high, jnp.where(lane == 1, middle, 0.0))
            out_refs[i][:, :columns] = sums.astype(BF16)
            out_refs[i][:, columns:] = jnp.where(lane == 2, low, lanes).astype(BF16)


def cache_projection(own, other, weights, width, model, added=(), finish=False, after=()):
    tokens, columns = own.shape[0], weights[0].shape[1]
    out = (tokens, columns // 2) if finish else (tokens // 2, columns + width)
    return resident_call(
        "cache_projection",
        functools.partial(cache_kernel, width, model, [half for _, half in added], finish),
        (),
        (own, other, *weights, *[array for array, _ in added]),
        [jax.ShapeDtypeStruct(out, BF16)] * 2,
        after,
    )


SIZES = (4, 2, 2, 2)
DEVICES = math.prod(SIZES)
DEPTH = SIZES[0]
PLACES = DEVICES // DEPTH


def swap(array, distance):
    return lax.ppermute(array, SEQ, [(i, i ^ distance) for i in range(DEVICES)])


def hop(array, steps):
    pairs = [
        (a * PLACES + i, b * PLACES + i) for a, b in sorted(steps.items()) for i in range(PLACES)
    ]
    return lax.ppermute(array, SEQ, pairs)


def shared_on_device(
    queries, keys, values, gate, residual, log_decay, out_weight, norm_gain, kv_weight
):
    tokens, heads = log_decay.shape
    width = queries.shape[1] // heads
    model = out_weight.shape[1]
    share = model // PLACES
    piece = share // DEPTH
    core = lax.axis_index("c")
    place = 4 * lax.axis_index("y") + 2 * lax.axis_index("x") + core

    with jax.named_scope("kv_weight_gather"):
        kv_mine = lax.all_gather(kv_weight, "z", axis=0, tiled=True)
    with jax.named_scope("out_weight_gather"):
        dealt = deal(out_weight, place, PLACES, piece)
        pieces = [swap(part, r) if r else part for r, part in enumerate(dealt)]

    running = jnp.cumsum(log_decay, axis=0)
    per = heads // PLACES
    within = running.reshape(tokens, PLACES, per).transpose(1, 0, 2)
    across = running.T.reshape(PLACES, per, tokens)
    states = local_states(keys, values, within, width, after=(dealt[0],))
    with jax.named_scope("state_scan"):
        parts = lax.all_to_all(states, PLANE, 0, 0, tiled=True)
    with jax.named_scope("residual_exchange"):
        dealt = spread(residual, PLACES, piece, after=(states,))
    with jax.named_scope("state_scan"):
        total = plane_total(parts, per, width, after=(dealt,))
        earlier = [hop(total, {a: a + d for a in range(DEPTH - d)}) for d in range(1, DEPTH)]
    with jax.named_scope("residual_exchange"):
        start = lax.all_to_all(hold(dealt, (total,)), PLANE, 0, 0, tiled=True)
        start = start.reshape(-1, share)
    intra, opened = local_intra(
        queries, keys, values, gate, within, across, width, after=(total,)
    )
    with jax.named_scope("state_scan"):
        prefix = plane_prefix(parts, earlier, width, after=(start, intra))
    with jax.named_scope("out_weight_gather"):
        shard = in_order(pieces, place, after=(kv_mine, total))
        out_full = lax.all_gather(shard, "z", axis=0, tiled=True)
    with jax.named_scope("state_scan"):
        entering = lax.all_to_all(hold(prefix, (shard,)), PLANE, 0, 0, tiled=True)
        entering = entering.reshape(heads, width, width)

    early, late = mix(queries, opened, intra, within, entering, width)

    with jax.named_scope("cache_weight"):
        gains = norm_gain.reshape(DEPTH, PLACES, piece)
        kv_full = []
        for r, rows in enumerate((kv_mine, swap(kv_mine, 1))):
            gain = lax.dynamic_index_in_dim(gains, place ^ r, 1, False).reshape(share, 1)
            kv_full.append((rows.astype(F32) * gain.astype(F32)).astype(BF16))

    def hidden_of(*halves, after=()):
        pieces = [(chip, half, (mixed, swap(mixed, 1))) for chip, half, mixed in halves]
        mine, theirs = out_projection(place, pieces, out_full, start, after)
        return mine, swap(theirs, 1)

    def share_of(hidden, added=(), finish=False, after=()):
        return cache_projection(*hidden, kv_full, width, model, added, finish, after)

    with jax.named_scope("projections"):
        early_x, late_y = swap(early, 2), swap(late, 4)
        early_far, late_far = swap(early_x, 4), swap(late_y, 2)
        home = hidden_of((0, 0, early), (0, 1, late), after=(early_x, late_y))
        near = hidden_of((1, 0, early_x), (2, 1, late_y), after=(home[0],))
        late_x = swap(hold(late, (near[0], early_far, late_far)), 2)
        early_y = swap(hold(early, (near[0], early_far, late_far)), 4)
        far = hidden_of((3, 0, early_far), (3, 1, late_far), after=(near[0],))
        early_far, late_far = share_of(far)
        early_x, late_y = share_of(near, after=(early_far,))
        late_x, early_y = hold(late_x, (early_x,)), hold(early_y, (early_x,))
        early_x, late_y = swap(early_x, 2), swap(late_y, 4)
        near = hidden_of((1, 1, late_x), (2, 0, early_y))
        late_x, early_y = share_of(
            near, [(swap(late_far, 4), 0), (swap(early_far, 2), 1)], after=(early_x, late_y)
        )
        late_x, early_y = swap(late_x, 2), swap(early_y, 4)
        added = [(early_x, 0), (late_x, 1), (early_y, 0), (late_y, 1)]
        return share_of(home, added, True)


def entering(part, axis, combine, identity):
    place = lax.axis_index(axis)
    gathered = jax.tree.map(lambda a: lax.all_gather(a, axis), part)
    state = jax.tree.map(lambda a, e: jnp.zeros_like(a) + jnp.asarray(e, a.dtype), part, identity)

    def one(step, state):
        return combine(
            state, jax.tree.map(lambda a: lax.dynamic_index_in_dim(a, step, 0, False), gathered)
        )

    return lax.fori_loop(0, place, one, state)


def local_retention(queries, keys, values, log_decay, block):
    tokens, heads, width = queries.shape
    count = tokens // block

    def to_blocks(array):
        return array.reshape((count, block) + array.shape[1:])

    lower = jnp.arange(block)[:, None] >= jnp.arange(block)[None, :]

    def advance(carry, inputs):
        state, offset = carry
        query_block, key_block, value_block, decay_block = inputs
        within = jnp.cumsum(decay_block, axis=0)
        spread = within[:, None, :] - within[None, :, :]
        factor = jnp.where(
            lower[:, :, None], jnp.exp(jnp.where(lower[:, :, None], spread, 0.0)), 0.0
        )
        scores = jnp.einsum(
            "ihd,jhd->hij", query_block, key_block, preferred_element_type=jnp.float32
        )
        weighted = scores * jnp.transpose(factor, (2, 0, 1))
        values_wide = value_block.astype(jnp.float32)
        intra = jnp.einsum("hij,jhd->ihd", weighted, values_wide, precision=HIGHEST)
        query_wide = query_block.astype(jnp.float32)
        carried = jnp.exp(within)[:, :, None] * jnp.einsum(
            "ihd,hde->ihe", query_wide, state, precision=HIGHEST
        )
        ending = within[-1]
        key_wide = key_block.astype(jnp.float32) * jnp.exp(ending[None, :] - within)[:, :, None]
        fresh = jnp.exp(ending)[:, None, None] * state + jnp.einsum(
            "jhd,jhe->hde", key_wide, values_wide, precision=HIGHEST
        )
        return ((fresh, offset + ending), (intra + carried, offset[None, :] + within))

    start = (jnp.zeros((heads, width, width), jnp.float32), jnp.zeros((heads,), jnp.float32))
    final, stacked = lax.scan(
        advance,
        start,
        (to_blocks(queries), to_blocks(keys), to_blocks(values), to_blocks(log_decay)),
    )
    return (
        stacked[0].reshape(tokens, heads, width),
        stacked[1].reshape(tokens, heads),
        final[0],
        final[1],
    )


def combine_states(earlier, later):
    return (earlier[0] * later[0], later[0][:, None, None] * earlier[1] + later[1])


def on_device(queries, keys, values, gate, residual, log_decay, out_weight, norm_gain, kv_weight):
    tokens = queries.shape[0]
    heads = log_decay.shape[1]
    width = queries.shape[1] // heads
    shaped = [array.reshape(tokens, heads, width) for array in (queries, keys, values)]
    partial_out, running, state, offset = local_retention(
        shaped[0], shaped[1], shaped[2], log_decay, min(512, tokens)
    )
    identity = (jnp.ones((heads,), jnp.float32), jnp.zeros((heads, width, width), jnp.float32))
    scan_decay, incoming = entering((jnp.exp(offset), state), "seq", combine_states, identity)
    retained = partial_out + jnp.exp(running)[:, :, None] * jnp.einsum(
        "thd,hde->the", shaped[0].astype(jnp.float32), incoming, precision=HIGHEST
    )
    scale = lax.rsqrt(jnp.mean(retained * retained, axis=2, keepdims=True) + 1e-06)
    mixed = (
        jax.nn.silu(gate.astype(jnp.float32)) * (retained * scale).reshape(tokens, heads * width)
    ).astype(jnp.bfloat16)
    all_heads = lax.all_gather(mixed, "head", axis=1, tiled=True)
    out_full, kv_full = (
        lax.all_gather(out_weight, "seq", axis=0, tiled=True),
        lax.all_gather(kv_weight, "seq", axis=0, tiled=True),
    )
    branch = jnp.dot(all_heads, out_full, preferred_element_type=jnp.float32)
    hidden = (residual.astype(jnp.float32) + branch).astype(jnp.bfloat16)
    wide = hidden.astype(jnp.float32)
    squares = lax.psum(jnp.sum(wide * wide, axis=1), "head")
    features = wide.shape[1] * lax.axis_size("head")
    inverse = lax.rsqrt(squares[:, None] / features + 1e-06)
    local_norm = (wide * inverse * norm_gain.astype(jnp.float32)[None, :]).astype(jnp.bfloat16)
    normalized = lax.all_gather(local_norm, "head", axis=1, tiled=True)
    projected = jnp.dot(normalized, kv_full, preferred_element_type=jnp.float32)
    cache_heads = kv_weight.shape[1] // (2 * width)
    arranged = projected.reshape(tokens, cache_heads, 2, width)
    cache_keys = arranged[:, :, 0, :].reshape(tokens, cache_heads * width).astype(jnp.bfloat16)
    cache_values = arranged[:, :, 1, :].reshape(tokens, cache_heads * width).astype(jnp.bfloat16)
    return (cache_keys, cache_values)


def solution(mesh):
    devices, split = mesh.shape["seq"], mesh.shape["head"]
    if split == 1 and devices == DEVICES:
        fine = Mesh(mesh.devices.reshape(SIZES + (1,)), SEQ + ("head",))
        placed, copied = P(SEQ, "head"), P("head")
        return jax.shard_map(
            shared_on_device,
            mesh=fine,
            in_specs=(placed,) * 7 + (copied, placed),
            out_specs=(placed, placed),
            check_vma=False,
        )
    placed = P("seq", "head")
    return jax.shard_map(
        on_device,
        mesh=mesh,
        in_specs=(placed,) * 7 + (P("head"), placed),
        out_specs=(placed, placed),
        check_vma=False,
    )
```

```python
import functools
import math

import jax
import jax.numpy as jnp
from jax import lax
from jax.experimental import pallas as pl
from jax.experimental.pallas import tpu as pltpu
from jax.sharding import Mesh
from jax.sharding import PartitionSpec as P

F32, BF16 = jnp.float32, jnp.bfloat16
HIGHEST = lax.Precision.HIGHEST
NORM_EPS = 1e-06
DECAY_ROWS = 16
PLANE = ("y", "x", "c")
SEQ = ("z", "y", "x", "c")
MIB = 1024 * 1024
VMEM_STREAMED = {"local_states": 60 * MIB, "local_intra": 54 * MIB, "mix": 16 * MIB}
VMEM_RESIDENT = 16 * MIB


def split_rows(total):
    high = total.astype(BF16).astype(F32)
    middle = (total - high).astype(BF16).astype(F32)
    low = total - high - middle
    row = lax.broadcasted_iota(jnp.int32, (DECAY_ROWS, total.shape[1]), 0)
    rows = jnp.where(row == 0, high, jnp.where(row == 1, middle, jnp.where(row == 2, low, 0.0)))
    return rows.astype(BF16)


def join_rows(rows):
    return jnp.sum(rows.astype(F32), axis=0, keepdims=True)


def dot(a, b, contract):
    return lax.dot_general(a, b, (contract, ((), ())), preferred_element_type=F32)


def state_kernel(width, key_ref, value_ref, within_ref, out_ref):
    tokens = key_ref.shape[0]
    within = within_ref[0]
    ending = within[tokens - 1 : tokens, :]
    fade = jnp.exp(ending - within)
    rows = width + DECAY_ROWS
    for head in range(within.shape[1]):
        columns = slice(head * width, (head + 1) * width)
        faded = (key_ref[:, columns].astype(F32) * fade[:, head : head + 1]).astype(BF16)
        state = dot(faded, value_ref[:, columns], ((0,), (0,)))
        out_ref[0, head * rows : head * rows + width, :] = state.astype(BF16)
        total = jnp.broadcast_to(ending[:, head : head + 1], (1, width))
        out_ref[0, head * rows + width : (head + 1) * rows, :] = split_rows(total)


def intra_kernel(
    width, query_ref, key_ref, value_ref, gate_ref, within_ref, across_ref, out_ref, open_ref
):
    tokens = query_ref.shape[0]
    within, across = within_ref[0], across_ref[0]
    lower = lax.broadcasted_iota(jnp.int32, (tokens, tokens), 0) >= lax.broadcasted_iota(
        jnp.int32, (tokens, tokens), 1
    )
    for head in range(within.shape[1]):
        columns = slice(head * width, (head + 1) * width)
        scores = dot(query_ref[:, columns], key_ref[:, columns], ((1,), (1,)))
        spread = within[:, head : head + 1] - across[head : head + 1, :]
        weighted = jnp.where(lower, scores * jnp.exp(jnp.where(lower, spread, 0.0)), 0.0)
        local = dot(weighted.astype(BF16), value_ref[:, columns], ((1,), (0,)))
        out_ref[:, columns] = local.astype(BF16)
        gate = gate_ref[:, columns].astype(F32)
        open_ref[:, columns] = (gate / (1.0 + jnp.exp(-gate))).astype(BF16)


def mix_kernel(width, query_ref, open_ref, intra_ref, within_ref, state_ref, *out_refs):
    reach = jnp.exp(within_ref[0])
    rows = out_refs[0].shape[0]
    for head in range(state_ref.shape[0]):
        columns = slice(head * width, (head + 1) * width)
        carried = dot(query_ref[:, columns], state_ref[head], ((1,), (0,)))
        retained = intra_ref[:, columns].astype(F32) + reach[:, head : head + 1] * carried
        scale = lax.rsqrt(jnp.mean(retained * retained, axis=1, keepdims=True) + NORM_EPS)
        mixed = (open_ref[:, columns].astype(F32) * (retained * scale)).astype(BF16)
        for half, out_ref in enumerate(out_refs):
            out_ref[:, columns] = mixed[half * rows : (half + 1) * rows]


def total_kernel(width, parts_ref, out_ref):
    for head in range(out_ref.shape[0]):
        top = head * (width + DECAY_ROWS)
        states, decays = slice(top, top + width), slice(top + width, top + width + DECAY_ROWS)
        state = jnp.zeros((width, width), F32)
        total = jnp.zeros((1, width), F32)
        for place in range(parts_ref.shape[0]):
            ending = join_rows(parts_ref[place, decays, :])
            state = jnp.exp(ending) * state + parts_ref[place, states, :].astype(F32)
            total = total + ending
        out_ref[head, :width, :] = state.astype(BF16)
        out_ref[head, width:, :] = split_rows(total)


def join_kernel(width, earlier_ref, later_ref, out_ref):
    for head in range(out_ref.shape[0]):
        ending = join_rows(later_ref[head, width:, :])
        state = jnp.exp(ending) * earlier_ref[head, :width, :].astype(F32)
        out_ref[head, :width, :] = (state + later_ref[head, :width, :].astype(F32)).astype(BF16)
        out_ref[head, width:, :] = split_rows(join_rows(earlier_ref[head, width:, :]) + ending)


def prefix_kernel(width, parts_ref, nearest_ref, others_ref, out_ref):
    for head in range(nearest_ref.shape[0]):
        top = head * (width + DECAY_ROWS)
        states, decays = slice(top, top + width), slice(top + width, top + width + DECAY_ROWS)
        reach = jnp.exp(join_rows(nearest_ref[head, width:, :]))
        state = reach * others_ref[head, :width, :].astype(F32)
        state = state + nearest_ref[head, :width, :].astype(F32)
        for place in range(parts_ref.shape[0]):
            out_ref[place, head] = state.astype(BF16)
            ending = join_rows(parts_ref[place, decays, :])
            state = jnp.exp(ending) * state + parts_ref[place, states, :].astype(F32)


def local_call(
    name, body, grid, operands, specs, out_specs, out_shape, scalars=(), scratch=(), after=()
):
    taken = len(scalars) + len(operands)

    def kernel(*refs):
        body(*refs[:taken], *refs[taken + len(after) :])

    return pl.pallas_call(
        kernel,
        grid_spec=pltpu.PrefetchScalarGridSpec(
            num_scalar_prefetch=len(scalars),
            grid=(grid,),
            in_specs=list(specs) + [pl.BlockSpec(memory_space=pltpu.HBM)] * len(after),
            out_specs=out_specs,
            scratch_shapes=scratch,
        ),
        out_shape=out_shape,
        compiler_params=pltpu.CompilerParams(vmem_limit_bytes=VMEM_STREAMED[name]),
        name=name,
    )(*scalars, *operands, *after)


def resident(count):
    return [pl.BlockSpec(memory_space=pltpu.VMEM)] * count


def resident_call(name, body, operands, out_shape, scalars=(), after=()):
    taken = len(scalars) + len(operands)

    def kernel(*refs):
        body(*refs[:taken], *refs[taken + len(after) :])

    return pl.pallas_call(
        kernel,
        in_specs=[pl.BlockSpec(memory_space=pltpu.SMEM)] * len(scalars)
        + resident(len(operands))
        + [pl.BlockSpec(memory_space=pltpu.HBM)] * len(after),
        out_specs=resident(len(out_shape)),
        out_shape=out_shape,
        compiler_params=pltpu.CompilerParams(vmem_limit_bytes=VMEM_RESIDENT),
        name=name,
    )(*scalars, *operands, *after)


def wide(rows, columns):
    return pl.BlockSpec((rows, columns), lambda i, *_: (0, i))


def whole(rows, columns):
    return pl.BlockSpec((rows, columns), lambda i, *_: (0, 0))


def group(*shape):
    return pl.BlockSpec((1,) + shape, lambda i, *_: (i, 0, 0))


def local_states(keys, values, within, width, after=()):
    tokens, groups, per = keys.shape[0], within.shape[0], within.shape[2]
    tall = per * (width + DECAY_ROWS)
    return local_call(
        "local_states",
        functools.partial(state_kernel, width),
        groups,
        (keys, values, within),
        (wide(tokens, per * width), wide(tokens, per * width), group(tokens, per)),
        group(tall, width),
        jax.ShapeDtypeStruct((groups, tall, width), BF16),
        after=after,
    )


def local_intra(queries, keys, values, gate, within, across, width, after=()):
    tokens, groups, per = keys.shape[0], within.shape[0], within.shape[2]
    heads = wide(tokens, per * width)
    return local_call(
        "local_intra",
        functools.partial(intra_kernel, width),
        groups,
        (queries, keys, values, gate, within, across),
        (heads, heads, heads, heads, group(tokens, per), group(per, tokens)),
        [heads, heads],
        [jax.ShapeDtypeStruct(queries.shape, BF16)] * 2,
        after=after,
    )


def mix(queries, opened, intra, within, states, width, after=()):
    groups, tokens, per = within.shape
    heads = wide(tokens, per * width)
    return local_call(
        "mix",
        functools.partial(mix_kernel, width),
        groups,
        (queries, opened, intra, within, states),
        (
            heads,
            heads,
            heads,
            group(tokens, per),
            pl.BlockSpec((per, width, width), lambda i: (i, 0, 0)),
        ),
        [wide(tokens // 2, per * width)] * 2,
        [jax.ShapeDtypeStruct((tokens // 2, queries.shape[1]), BF16)] * 2,
        after=after,
    )


def plane_total(parts, heads, width, after=()):
    shape = jax.ShapeDtypeStruct((heads, width + DECAY_ROWS, width), BF16)
    body = functools.partial(total_kernel, width)
    return resident_call("plane_total", body, (parts,), [shape], after=after)[0]


def join(earlier, later, width, after=()):
    shape = jax.ShapeDtypeStruct(later.shape, BF16)
    body = functools.partial(join_kernel, width)
    return resident_call("join", body, (earlier, later), [shape], after=after)[0]


def plane_prefix(parts, nearest, others, width, after=()):
    shape = jax.ShapeDtypeStruct((parts.shape[0], nearest.shape[0], width, width), BF16)
    body = functools.partial(prefix_kernel, width)
    return resident_call("plane_prefix", body, (parts, nearest, others), [shape], after=after)[0]


def deal_kernel(ways, block, place_ref, *refs):
    *source_refs, even_ref, odd_ref = refs
    for r in range(ways):
        target_ref, top = (even_ref, odd_ref)[r % 2], 0
        for source_ref in source_refs:
            rows = slice(top, top + source_ref.shape[0])
            for i in range(target_ref.shape[2] // block):
                start = pl.multiple_of((i * ways + (place_ref[0] ^ r)) * block, block)
                columns = slice(i * block, (i + 1) * block)
                target_ref[r // 2, rows, columns] = source_ref[:, pl.ds(start, block)]
            top += source_ref.shape[0]


def deal(arrays, place, ways, block, after=()):
    rows = sum(array.shape[0] for array in arrays)
    shape = jax.ShapeDtypeStruct((ways // 2, rows, arrays[0].shape[1] // ways), BF16)
    return resident_call(
        "deal",
        functools.partial(deal_kernel, ways, block),
        arrays,
        [shape, shape],
        scalars=(place.reshape(1),),
        after=after,
    )


def pair_kernel(heights, even_ref, odd_ref, *target_refs):
    chips = even_ref.shape[0]
    for i, target_ref in enumerate(target_refs):
        top = sum(heights[: i // chips])
        rows = slice(top, top + heights[i // chips])
        target_ref[0] = even_ref[i % chips, rows, :]
        target_ref[1] = odd_ref[i % chips, rows, :]


def pair(even, odd, heights, after=()):
    chips, _, columns = even.shape
    shapes = [jax.ShapeDtypeStruct((2, rows, columns), even.dtype) for rows in heights]
    body = functools.partial(pair_kernel, heights)
    pairs = resident_call(
        "pair", body, (even, odd), [s for s in shapes for _ in range(chips)], after=after
    )
    return [pairs[i : i + chips] for i in range(0, len(pairs), chips)]


def order_kernel(place_ref, *refs):
    *sources, target_ref = refs
    rows = sources[0].shape[1]
    for r in range(2 * len(sources)):
        start = pl.multiple_of((place_ref[0] ^ r) * rows, rows)
        target_ref[pl.ds(start, rows), :] = sources[r // 2][r % 2]


def in_order(arrays, place, after=()):
    _, rows, columns = arrays[0].shape
    tall = (2 * len(arrays) * rows, columns)
    return resident_call(
        "in_order",
        order_kernel,
        arrays,
        [jax.ShapeDtypeStruct(tall, arrays[0].dtype)],
        scalars=(place.reshape(1),),
        after=after,
    )[0]


def hold(arrays, after):
    kept, count = pl.BlockSpec(memory_space=pltpu.HBM), len(arrays)
    return pl.pallas_call(
        lambda *refs: None,
        in_specs=[kept] * (count + len(after)),
        out_specs=[kept] * count,
        out_shape=[jax.ShapeDtypeStruct(array.shape, array.dtype) for array in arrays],
        input_output_aliases={i: i for i in range(count)},
        compiler_params=pltpu.CompilerParams(vmem_limit_bytes=VMEM_RESIDENT),
        name="hold",
    )(*arrays, *after)


def out_kernel(halves, *refs):
    chips, pieces = len(halves), 2 * len(halves)
    mixed, weight_ref, start_refs = refs[:pieces], refs[pieces], refs[pieces + 1 : -2]
    tokens, depth = mixed[0].shape
    step = min(depth, 512)
    total = jnp.zeros((pieces * tokens, weight_ref.shape[1]), F32)
    for start in range(0, depth, step):
        left = jnp.concatenate([ref[:, start : start + step] for ref in mixed], axis=0)
        total = total + dot(left, weight_ref[start : start + step, :], ((1,), (0,)))
    for chip in range(chips):
        rows = slice(halves[chip] * tokens, (halves[chip] + 1) * tokens)
        for core, out_ref in enumerate(refs[-2:]):
            i = 2 * chip + core
            hidden = start_refs[chip][core, rows, :].astype(F32)
            hidden = hidden + total[i * tokens : (i + 1) * tokens]
            out_ref[chip * tokens : (chip + 1) * tokens, :] = hidden.astype(BF16)


def out_projection(pieces, weight, after=()):
    halves, mixed, starts = zip(*pieces)
    mixed = [array for cores in mixed for array in cores]
    shape = jax.ShapeDtypeStruct((len(pieces) * mixed[0].shape[0], weight.shape[1]), BF16)
    return resident_call(
        "out_projection",
        functools.partial(out_kernel, halves),
        (*mixed, weight, *starts),
        [shape, shape],
        after=after,
    )


def cache_kernel(width, model, joined, finish, *refs):
    own_ref, other_ref, own_weight_ref, other_weight_ref, *refs = refs
    added, out_refs = refs[: len(joined)], refs[len(joined) :]
    tokens, columns = own_ref.shape[0] // 2, own_weight_ref.shape[1]
    own, other = own_ref[...], other_ref[...]
    total = dot(own, own_weight_ref[...], ((1,), (0,)))
    total = total + dot(other, other_weight_ref[...], ((1,), (0,)))
    squares = jnp.square(own.astype(F32)) + jnp.square(other.astype(F32))
    squares = jnp.sum(squares, axis=1, keepdims=True)
    for i in range(2):
        rows = slice(i * tokens, (i + 1) * tokens)
        sums, norm = total[rows], squares[rows]
        for ref, half in zip(added, joined):
            if half == i:
                sums = sums + ref[:, :columns].astype(F32)
                norm = norm + jnp.sum(ref[:, columns:].astype(F32), axis=1, keepdims=True)
        if finish:
            sums = (sums * lax.rsqrt(norm / model + NORM_EPS)).astype(BF16)
            for head in range(columns // (2 * width)):
                for kind, out_ref in enumerate(out_refs):
                    start = (2 * head + kind) * width
                    out_ref[rows, head * width : (head + 1) * width] = sums[:, start : start + width]
        else:
            high = norm.astype(BF16).astype(F32)
            middle = (norm - high).astype(BF16).astype(F32)
            low = norm - high - middle
            lane = lax.broadcasted_iota(jnp.int32, (tokens, width), 1)
            lanes = jnp.where(lane == 0, high, jnp.where(lane == 1, middle, 0.0))
            out_refs[i][:, :columns] = sums.astype(BF16)
            out_refs[i][:, columns:] = jnp.where(lane == 2, low, lanes).astype(BF16)


def cache_projection(own, other, weights, width, model, added=(), finish=False, after=()):
    tokens, columns = own.shape[0], weights[0].shape[1]
    out = (tokens, columns // 2) if finish else (tokens // 2, columns + width)
    return resident_call(
        "cache_projection",
        functools.partial(cache_kernel, width, model, [half for _, half in added], finish),
        (own, other, *weights, *[array for array, _ in added]),
        [jax.ShapeDtypeStruct(out, BF16)] * 2,
        after=after,
    )


SIZES = (4, 2, 2, 2)
DEVICES = math.prod(SIZES)
DEPTH = SIZES[0]
PLACES = DEVICES // DEPTH


def swap(array, distance):
    return lax.ppermute(array, SEQ, [(i, i ^ distance) for i in range(DEVICES)])


def hop(array, steps):
    pairs = [
        (a * PLACES + i, b * PLACES + i) for a, b in sorted(steps.items()) for i in range(PLACES)
    ]
    return lax.ppermute(array, SEQ, pairs)


def shared_on_device(
    queries, keys, values, gate, residual, log_decay, out_weight, norm_gain, kv_weight
):
    tokens, heads = log_decay.shape
    width = queries.shape[1] // heads
    model = out_weight.shape[1]
    share = model // PLACES
    piece = share // DEPTH
    core = lax.axis_index("c")
    place = 4 * lax.axis_index("y") + 2 * lax.axis_index("x") + core

    with jax.named_scope("kv_weight_gather"):
        kv_mine = lax.all_gather(kv_weight, "z", axis=0, tiled=True)
    running = jnp.cumsum(log_decay, axis=0)
    per = heads // PLACES
    within = running.reshape(tokens, PLACES, per).transpose(1, 0, 2)
    across = running.T.reshape(PLACES, per, tokens)
    states = local_states(keys, values, within, width)
    with jax.named_scope("state_scan"):
        parts = lax.all_to_all(states, PLANE, 0, 0, tiled=True)

    intra, opened = local_intra(
        queries, keys, values, gate, within, across, width, after=(states,)
    )
    with jax.named_scope("state_scan"):
        total = plane_total(parts, per, width, after=(intra,))
        nearest = hop(total, {a: a + 1 for a in range(DEPTH - 1)})
        joined = join(nearest, total, width)
        others = hop(joined, {a: a + 2 for a in range(DEPTH - 2)})

    def exchange(pairs):
        return [swap(part, 2 * chip) if chip else part for chip, part in enumerate(pairs)]

    even, odd = deal((residual, out_weight), place, PLACES, piece, after=(total,))
    starts, weights = pair(even, swap(odd, 1), (tokens, out_weight.shape[0]))
    with jax.named_scope("out_weight_gather"):
        shard = in_order(exchange(weights), place, after=(joined,))
        out_full = lax.all_gather(*hold((shard,), (kv_mine,)), "z", axis=0, tiled=True)
    with jax.named_scope("residual_exchange"):
        starts = exchange(hold(starts, (shard,)))
    with jax.named_scope("state_scan"):
        prefix = plane_prefix(parts, nearest, others, width, after=(kv_mine, shard))
        entering = lax.all_to_all(prefix, PLANE, 0, 0, tiled=True)
        entering = entering.reshape(heads, width, width)

    early, late = mix(queries, opened, intra, within, entering, width)
    early, late = hold((early, late), tuple(starts[1:]))

    with jax.named_scope("cache_weight"):
        gains = norm_gain.reshape(DEPTH, PLACES, piece)
        kv_full = []
        for r, rows in enumerate((kv_mine, swap(kv_mine, 1))):
            gain = lax.dynamic_index_in_dim(gains, place ^ r, 1, False).reshape(share, 1)
            kv_full.append((rows.astype(F32) * gain.astype(F32)).astype(BF16))

    def hidden_of(*halves, after=()):
        pieces = [(half, (mixed, swap(mixed, 1)), starts[chip]) for chip, half, mixed in halves]
        mine, theirs = out_projection(pieces, out_full, after)
        return mine, swap(theirs, 1)

    def share_of(hidden, added=(), finish=False, after=()):
        return cache_projection(*hidden, kv_full, width, model, added, finish, after)

    with jax.named_scope("projections"):
        early_x, late_y = swap(early, 2), swap(late, 4)
        early_far, late_far = swap(early_x, 4), swap(late_y, 2)
        near = hidden_of((1, 0, early_x), (2, 1, late_y))
        early, late = hold((early, late), (early_far, late_far))
        late_x, early_y = swap(late, 2), swap(early, 4)
        far = hidden_of((3, 0, early_far), (3, 1, late_far), after=(near[0],))
        early_far, late_far = share_of(far)
        early_x, late_y = share_of(near, after=(early_far,))
        late_x, early_y = hold((late_x, early_y), (early_x,))
        early_x, late_y = swap(early_x, 2), swap(late_y, 4)
        late_far, early_far = swap(late_far, 4), swap(early_far, 2)
        near = hidden_of((1, 1, late_x), (2, 0, early_y))
        late_x, early_y = share_of(near, [(late_far, 0), (early_far, 1)])
        home = hidden_of((0, 0, early), (0, 1, late), after=(late_x, early_x, late_y))
        late_x, early_y = swap(late_x, 2), swap(early_y, 4)
        added = [(early_x, 0), (late_x, 1), (early_y, 0), (late_y, 1)]
        return share_of(home, added, True)


def entering(part, axis, combine, identity):
    place = lax.axis_index(axis)
    gathered = jax.tree.map(lambda a: lax.all_gather(a, axis), part)
    state = jax.tree.map(lambda a, e: jnp.zeros_like(a) + jnp.asarray(e, a.dtype), part, identity)

    def one(step, state):
        return combine(
            state, jax.tree.map(lambda a: lax.dynamic_index_in_dim(a, step, 0, False), gathered)
        )

    return lax.fori_loop(0, place, one, state)


def local_retention(queries, keys, values, log_decay, block):
    tokens, heads, width = queries.shape
    count = tokens // block

    def to_blocks(array):
        return array.reshape((count, block) + array.shape[1:])

    lower = jnp.arange(block)[:, None] >= jnp.arange(block)[None, :]

    def advance(carry, inputs):
        state, offset = carry
        query_block, key_block, value_block, decay_block = inputs
        within = jnp.cumsum(decay_block, axis=0)
        spread = within[:, None, :] - within[None, :, :]
        factor = jnp.where(
            lower[:, :, None], jnp.exp(jnp.where(lower[:, :, None], spread, 0.0)), 0.0
        )
        scores = jnp.einsum(
            "ihd,jhd->hij", query_block, key_block, preferred_element_type=jnp.float32
        )
        weighted = scores * jnp.transpose(factor, (2, 0, 1))
        values_wide = value_block.astype(jnp.float32)
        intra = jnp.einsum("hij,jhd->ihd", weighted, values_wide, precision=HIGHEST)
        query_wide = query_block.astype(jnp.float32)
        carried = jnp.exp(within)[:, :, None] * jnp.einsum(
            "ihd,hde->ihe", query_wide, state, precision=HIGHEST
        )
        ending = within[-1]
        key_wide = key_block.astype(jnp.float32) * jnp.exp(ending[None, :] - within)[:, :, None]
        fresh = jnp.exp(ending)[:, None, None] * state + jnp.einsum(
            "jhd,jhe->hde", key_wide, values_wide, precision=HIGHEST
        )
        return ((fresh, offset + ending), (intra + carried, offset[None, :] + within))

    start = (jnp.zeros((heads, width, width), jnp.float32), jnp.zeros((heads,), jnp.float32))
    final, stacked = lax.scan(
        advance,
        start,
        (to_blocks(queries), to_blocks(keys), to_blocks(values), to_blocks(log_decay)),
    )
    return (
        stacked[0].reshape(tokens, heads, width),
        stacked[1].reshape(tokens, heads),
        final[0],
        final[1],
    )


def combine_states(earlier, later):
    return (earlier[0] * later[0], later[0][:, None, None] * earlier[1] + later[1])


def on_device(queries, keys, values, gate, residual, log_decay, out_weight, norm_gain, kv_weight):
    tokens = queries.shape[0]
    heads = log_decay.shape[1]
    width = queries.shape[1] // heads
    shaped = [array.reshape(tokens, heads, width) for array in (queries, keys, values)]
    partial_out, running, state, offset = local_retention(
        shaped[0], shaped[1], shaped[2], log_decay, min(512, tokens)
    )
    identity = (jnp.ones((heads,), jnp.float32), jnp.zeros((heads, width, width), jnp.float32))
    scan_decay, incoming = entering((jnp.exp(offset), state), "seq", combine_states, identity)
    retained = partial_out + jnp.exp(running)[:, :, None] * jnp.einsum(
        "thd,hde->the", shaped[0].astype(jnp.float32), incoming, precision=HIGHEST
    )
    scale = lax.rsqrt(jnp.mean(retained * retained, axis=2, keepdims=True) + 1e-06)
    mixed = (
        jax.nn.silu(gate.astype(jnp.float32)) * (retained * scale).reshape(tokens, heads * width)
    ).astype(jnp.bfloat16)
    all_heads = lax.all_gather(mixed, "head", axis=1, tiled=True)
    out_full, kv_full = (
        lax.all_gather(out_weight, "seq", axis=0, tiled=True),
        lax.all_gather(kv_weight, "seq", axis=0, tiled=True),
    )
    branch = jnp.dot(all_heads, out_full, preferred_element_type=jnp.float32)
    hidden = (residual.astype(jnp.float32) + branch).astype(jnp.bfloat16)
    wide = hidden.astype(jnp.float32)
    squares = lax.psum(jnp.sum(wide * wide, axis=1), "head")
    features = wide.shape[1] * lax.axis_size("head")
    inverse = lax.rsqrt(squares[:, None] / features + 1e-06)
    local_norm = (wide * inverse * norm_gain.astype(jnp.float32)[None, :]).astype(jnp.bfloat16)
    normalized = lax.all_gather(local_norm, "head", axis=1, tiled=True)
    projected = jnp.dot(normalized, kv_full, preferred_element_type=jnp.float32)
    cache_heads = kv_weight.shape[1] // (2 * width)
    arranged = projected.reshape(tokens, cache_heads, 2, width)
    cache_keys = arranged[:, :, 0, :].reshape(tokens, cache_heads * width).astype(jnp.bfloat16)
    cache_values = arranged[:, :, 1, :].reshape(tokens, cache_heads * width).astype(jnp.bfloat16)
    return (cache_keys, cache_values)


def solution(mesh):
    devices, split = mesh.shape["seq"], mesh.shape["head"]
    if split == 1 and devices == DEVICES:
        fine = Mesh(mesh.devices.reshape(SIZES + (1,)), SEQ + ("head",))
        placed, copied = P(SEQ, "head"), P("head")
        return jax.shard_map(
            shared_on_device,
            mesh=fine,
            in_specs=(placed,) * 7 + (copied, placed),
            out_specs=(placed, placed),
            check_vma=False,
        )
    placed = P("seq", "head")
    return jax.shard_map(
        on_device,
        mesh=mesh,
        in_specs=(placed,) * 7 + (P("head"), placed),
        out_specs=(placed, placed),
        check_vma=False,
    )
```

```python
import functools
import math

import jax
import jax.numpy as jnp
from jax import lax
from jax.experimental import pallas as pl
from jax.experimental.pallas import tpu as pltpu
from jax.sharding import Mesh
from jax.sharding import PartitionSpec as P

F32, BF16 = jnp.float32, jnp.bfloat16
HIGHEST = lax.Precision.HIGHEST
NORM_EPS = 1e-06
DECAY_ROWS = 16
PLANE = ("y", "x", "c")
SEQ = ("z", "y", "x", "c")
MIB = 1024 * 1024
VMEM_STREAMED = {"local_states": 60 * MIB, "local_intra": 54 * MIB, "mix": 60 * MIB}
VMEM_RESIDENT = 16 * MIB


def split_rows(total):
    high = total.astype(BF16).astype(F32)
    middle = (total - high).astype(BF16).astype(F32)
    low = total - high - middle
    row = lax.broadcasted_iota(jnp.int32, (DECAY_ROWS, total.shape[1]), 0)
    rows = jnp.where(row == 0, high, jnp.where(row == 1, middle, jnp.where(row == 2, low, 0.0)))
    return rows.astype(BF16)


def join_rows(rows):
    return jnp.sum(rows.astype(F32), axis=0, keepdims=True)


def dot(a, b, contract):
    return lax.dot_general(a, b, (contract, ((), ())), preferred_element_type=F32)


def state_kernel(width, key_ref, value_ref, decay_ref, out_ref, fade_ref, ending_ref):
    tokens = key_ref.shape[0]
    groups, _, per = fade_ref.shape

    @pl.when(pl.program_id(0) == 0)
    def _():
        decay = decay_ref[...]
        later = lax.broadcasted_iota(jnp.int32, (tokens, tokens), 0) < lax.broadcasted_iota(
            jnp.int32, (tokens, tokens), 1
        )
        rest = lax.dot_general(
            later.astype(F32),
            decay,
            (((1,), (0,)), ((), ())),
            precision=HIGHEST,
            preferred_element_type=F32,
        )
        fade = jnp.exp(rest)
        ending = rest[:1] + decay[:1]
        for i in range(groups):
            fade_ref[i] = fade[:, i * per : (i + 1) * per]
            ending_ref[i] = ending[:, i * per : (i + 1) * per]

    rows = width + DECAY_ROWS
    for i in range(out_ref.shape[0]):
        place = pl.program_id(0) * out_ref.shape[0] + i
        fade, ending = fade_ref[place], ending_ref[place]
        for head in range(per):
            columns = slice((i * per + head) * width, (i * per + head + 1) * width)
            faded = (key_ref[:, columns].astype(F32) * fade[:, head : head + 1]).astype(BF16)
            state = dot(faded, value_ref[:, columns], ((0,), (0,)))
            out_ref[i, head * rows : head * rows + width, :] = state.astype(BF16)
            total = jnp.broadcast_to(ending[:, head : head + 1], (1, width))
            out_ref[i, head * rows + width : (head + 1) * rows, :] = split_rows(total)


def intra_kernel(
    width, query_ref, key_ref, value_ref, gate_ref, within_ref, across_ref, out_ref, open_ref
):
    tokens = query_ref.shape[0]
    within, across = within_ref[0], across_ref[0]
    lower = lax.broadcasted_iota(jnp.int32, (tokens, tokens), 0) >= lax.broadcasted_iota(
        jnp.int32, (tokens, tokens), 1
    )
    for head in range(within.shape[1]):
        columns = slice(head * width, (head + 1) * width)
        scores = dot(query_ref[:, columns], key_ref[:, columns], ((1,), (1,)))
        spread = within[:, head : head + 1] - across[head : head + 1, :]
        weighted = jnp.where(lower, scores * jnp.exp(jnp.where(lower, spread, 0.0)), 0.0)
        local = dot(weighted.astype(BF16), value_ref[:, columns], ((1,), (0,)))
        out_ref[:, columns] = local.astype(BF16)
        gate = gate_ref[:, columns].astype(F32)
        open_ref[:, columns] = (gate / (1.0 + jnp.exp(-gate))).astype(BF16)


def mix_kernel(width, query_ref, open_ref, intra_ref, within_ref, state_ref, *out_refs):
    reach = jnp.exp(within_ref[0])
    rows = out_refs[0].shape[0]
    for head in range(state_ref.shape[0]):
        columns = slice(head * width, (head + 1) * width)
        carried = dot(query_ref[:, columns], state_ref[head], ((1,), (0,)))
        retained = intra_ref[:, columns].astype(F32) + reach[:, head : head + 1] * carried
        scale = lax.rsqrt(jnp.mean(retained * retained, axis=1, keepdims=True) + NORM_EPS)
        mixed = (open_ref[:, columns].astype(F32) * (retained * scale)).astype(BF16)
        for half, out_ref in enumerate(out_refs):
            out_ref[:, columns] = mixed[half * rows : (half + 1) * rows]


def total_kernel(width, parts_ref, out_ref):
    for head in range(out_ref.shape[0]):
        top = head * (width + DECAY_ROWS)
        states, decays = slice(top, top + width), slice(top + width, top + width + DECAY_ROWS)
        state = jnp.zeros((width, width), F32)
        total = jnp.zeros((1, width), F32)
        for place in range(parts_ref.shape[0]):
            ending = join_rows(parts_ref[place, decays, :])
            state = jnp.exp(ending) * state + parts_ref[place, states, :].astype(F32)
            total = total + ending
        out_ref[head, :width, :] = state.astype(BF16)
        out_ref[head, width:, :] = split_rows(total)


def join_kernel(width, earlier_ref, later_ref, out_ref):
    for head in range(out_ref.shape[0]):
        ending = join_rows(later_ref[head, width:, :])
        state = jnp.exp(ending) * earlier_ref[head, :width, :].astype(F32)
        out_ref[head, :width, :] = (state + later_ref[head, :width, :].astype(F32)).astype(BF16)
        out_ref[head, width:, :] = split_rows(join_rows(earlier_ref[head, width:, :]) + ending)


def prefix_kernel(width, parts_ref, nearest_ref, others_ref, out_ref):
    for head in range(nearest_ref.shape[0]):
        top = head * (width + DECAY_ROWS)
        states, decays = slice(top, top + width), slice(top + width, top + width + DECAY_ROWS)
        reach = jnp.exp(join_rows(nearest_ref[head, width:, :]))
        state = reach * others_ref[head, :width, :].astype(F32)
        state = state + nearest_ref[head, :width, :].astype(F32)
        for place in range(parts_ref.shape[0]):
            out_ref[place, head] = state.astype(BF16)
            ending = join_rows(parts_ref[place, decays, :])
            state = jnp.exp(ending) * state + parts_ref[place, states, :].astype(F32)


def local_call(
    name, body, grid, operands, specs, out_specs, out_shape, scalars=(), scratch=(), after=()
):
    taken = len(scalars) + len(operands)

    def kernel(*refs):
        body(*refs[:taken], *refs[taken + len(after) :])

    return pl.pallas_call(
        kernel,
        grid_spec=pltpu.PrefetchScalarGridSpec(
            num_scalar_prefetch=len(scalars),
            grid=(grid,),
            in_specs=list(specs) + [pl.BlockSpec(memory_space=pltpu.HBM)] * len(after),
            out_specs=out_specs,
            scratch_shapes=scratch,
        ),
        out_shape=out_shape,
        compiler_params=pltpu.CompilerParams(vmem_limit_bytes=VMEM_STREAMED[name]),
        name=name,
    )(*scalars, *operands, *after)


def resident(count):
    return [pl.BlockSpec(memory_space=pltpu.VMEM)] * count


def resident_call(name, body, operands, out_shape, scalars=(), after=()):
    taken = len(scalars) + len(operands)

    def kernel(*refs):
        body(*refs[:taken], *refs[taken + len(after) :])

    return pl.pallas_call(
        kernel,
        in_specs=[pl.BlockSpec(memory_space=pltpu.SMEM)] * len(scalars)
        + resident(len(operands))
        + [pl.BlockSpec(memory_space=pltpu.HBM)] * len(after),
        out_specs=resident(len(out_shape)),
        out_shape=out_shape,
        compiler_params=pltpu.CompilerParams(vmem_limit_bytes=VMEM_RESIDENT),
        name=name,
    )(*scalars, *operands, *after)


def wide(rows, columns):
    return pl.BlockSpec((rows, columns), lambda i, *_: (0, i))


def whole(rows, columns):
    return pl.BlockSpec((rows, columns), lambda i, *_: (0, 0))


def group(*shape):
    return pl.BlockSpec((1,) + shape, lambda i, *_: (i, 0, 0))


def local_states(keys, values, log_decay, groups, width, after=()):
    tokens, heads = log_decay.shape
    per, steps = heads // groups, groups // 2
    tall = per * (width + DECAY_ROWS)
    wider = wide(tokens, 2 * per * width)
    return local_call(
        "local_states",
        functools.partial(state_kernel, width),
        steps,
        (keys, values, log_decay),
        (wider, wider, whole(tokens, heads)),
        pl.BlockSpec((2, tall, width), lambda i: (i, 0, 0)),
        jax.ShapeDtypeStruct((groups, tall, width), BF16),
        scratch=(pltpu.VMEM((groups, tokens, per), F32), pltpu.VMEM((groups, 1, per), F32)),
        after=after,
    )


def local_intra(queries, keys, values, gate, within, across, width, after=()):
    tokens, groups, per = keys.shape[0], within.shape[0], within.shape[2]
    heads = wide(tokens, per * width)
    return local_call(
        "local_intra",
        functools.partial(intra_kernel, width),
        groups,
        (queries, keys, values, gate, within, across),
        (heads, heads, heads, heads, group(tokens, per), group(per, tokens)),
        [heads, heads],
        [jax.ShapeDtypeStruct(queries.shape, BF16)] * 2,
        after=after,
    )


def mix(queries, opened, intra, within, states, width, after=()):
    groups, tokens, per = within.shape
    heads = wide(tokens, per * width)
    return local_call(
        "mix",
        functools.partial(mix_kernel, width),
        groups,
        (queries, opened, intra, within, states),
        (
            heads,
            heads,
            heads,
            group(tokens, per),
            pl.BlockSpec((per, width, width), lambda i: (i, 0, 0)),
        ),
        [wide(tokens // 2, per * width)] * 2,
        [jax.ShapeDtypeStruct((tokens // 2, queries.shape[1]), BF16)] * 2,
        after=after,
    )


def plane_total(parts, heads, width, after=()):
    shape = jax.ShapeDtypeStruct((heads, width + DECAY_ROWS, width), BF16)
    body = functools.partial(total_kernel, width)
    return resident_call("plane_total", body, (parts,), [shape], after=after)[0]


def join(earlier, later, width, after=()):
    shape = jax.ShapeDtypeStruct(later.shape, BF16)
    body = functools.partial(join_kernel, width)
    return resident_call("join", body, (earlier, later), [shape], after=after)[0]


def plane_prefix(parts, nearest, others, width, after=()):
    shape = jax.ShapeDtypeStruct((parts.shape[0], nearest.shape[0], width, width), BF16)
    body = functools.partial(prefix_kernel, width)
    return resident_call("plane_prefix", body, (parts, nearest, others), [shape], after=after)[0]


def deal_kernel(ways, block, place_ref, *refs):
    *source_refs, even_ref, odd_ref = refs
    for r in range(ways):
        target_ref, top = (even_ref, odd_ref)[r % 2], 0
        for source_ref in source_refs:
            rows = slice(top, top + source_ref.shape[0])
            for i in range(target_ref.shape[2] // block):
                start = pl.multiple_of((i * ways + (place_ref[0] ^ r)) * block, block)
                columns = slice(i * block, (i + 1) * block)
                target_ref[r // 2, rows, columns] = source_ref[:, pl.ds(start, block)]
            top += source_ref.shape[0]


def deal(arrays, place, ways, block, after=()):
    rows = sum(array.shape[0] for array in arrays)
    shape = jax.ShapeDtypeStruct((ways // 2, rows, arrays[0].shape[1] // ways), BF16)
    return resident_call(
        "deal",
        functools.partial(deal_kernel, ways, block),
        arrays,
        [shape, shape],
        scalars=(place.reshape(1),),
        after=after,
    )


def pair_kernel(heights, even_ref, odd_ref, *target_refs):
    chips = even_ref.shape[0]
    for i, target_ref in enumerate(target_refs):
        top = sum(heights[: i // chips])
        rows = slice(top, top + heights[i // chips])
        target_ref[0] = even_ref[i % chips, rows, :]
        target_ref[1] = odd_ref[i % chips, rows, :]


def pair(even, odd, heights, after=()):
    chips, _, columns = even.shape
    shapes = [jax.ShapeDtypeStruct((2, rows, columns), even.dtype) for rows in heights]
    body = functools.partial(pair_kernel, heights)
    pairs = resident_call(
        "pair", body, (even, odd), [s for s in shapes for _ in range(chips)], after=after
    )
    return [pairs[i : i + chips] for i in range(0, len(pairs), chips)]


def order_kernel(place_ref, *refs):
    *sources, target_ref = refs
    rows = sources[0].shape[1]
    for r in range(2 * len(sources)):
        start = pl.multiple_of((place_ref[0] ^ r) * rows, rows)
        target_ref[pl.ds(start, rows), :] = sources[r // 2][r % 2]


def in_order(arrays, place, after=()):
    _, rows, columns = arrays[0].shape
    tall = (2 * len(arrays) * rows, columns)
    return resident_call(
        "in_order",
        order_kernel,
        arrays,
        [jax.ShapeDtypeStruct(tall, arrays[0].dtype)],
        scalars=(place.reshape(1),),
        after=after,
    )[0]


def hold(arrays, after):
    kept, count = pl.BlockSpec(memory_space=pltpu.HBM), len(arrays)
    return pl.pallas_call(
        lambda *refs: None,
        in_specs=[kept] * (count + len(after)),
        out_specs=[kept] * count,
        out_shape=[jax.ShapeDtypeStruct(array.shape, array.dtype) for array in arrays],
        input_output_aliases={i: i for i in range(count)},
        compiler_params=pltpu.CompilerParams(vmem_limit_bytes=VMEM_RESIDENT),
        name="hold",
    )(*arrays, *after)


def out_kernel(halves, *refs):
    chips, pieces = len(halves), 2 * len(halves)
    mixed, weight_ref, start_refs = refs[:pieces], refs[pieces], refs[pieces + 1 : -2]
    tokens, depth = mixed[0].shape
    step = min(depth, 512)
    total = jnp.zeros((pieces * tokens, weight_ref.shape[1]), F32)
    for start in range(0, depth, step):
        left = jnp.concatenate([ref[:, start : start + step] for ref in mixed], axis=0)
        total = total + dot(left, weight_ref[start : start + step, :], ((1,), (0,)))
    for chip in range(chips):
        rows = slice(halves[chip] * tokens, (halves[chip] + 1) * tokens)
        for core, out_ref in enumerate(refs[-2:]):
            i = 2 * chip + core
            hidden = start_refs[chip][core, rows, :].astype(F32)
            hidden = hidden + total[i * tokens : (i + 1) * tokens]
            out_ref[chip * tokens : (chip + 1) * tokens, :] = hidden.astype(BF16)


def out_projection(pieces, weight, after=()):
    halves, mixed, starts = zip(*pieces)
    mixed = [array for cores in mixed for array in cores]
    shape = jax.ShapeDtypeStruct((len(pieces) * mixed[0].shape[0], weight.shape[1]), BF16)
    return resident_call(
        "out_projection",
        functools.partial(out_kernel, halves),
        (*mixed, weight, *starts),
        [shape, shape],
        after=after,
    )


def cache_kernel(width, model, joined, finish, *refs):
    own_ref, other_ref, own_weight_ref, other_weight_ref, *refs = refs
    added, out_refs = refs[: len(joined)], refs[len(joined) :]
    tokens, columns = own_ref.shape[0] // 2, own_weight_ref.shape[1]
    own, other = own_ref[...], other_ref[...]
    total = dot(own, own_weight_ref[...], ((1,), (0,)))
    total = total + dot(other, other_weight_ref[...], ((1,), (0,)))
    squares = jnp.square(own.astype(F32)) + jnp.square(other.astype(F32))
    squares = jnp.sum(squares, axis=1, keepdims=True)
    for i in range(2):
        rows = slice(i * tokens, (i + 1) * tokens)
        sums, norm = total[rows], squares[rows]
        for ref, half in zip(added, joined):
            if half == i:
                sums = sums + ref[:, :columns].astype(F32)
                norm = norm + jnp.sum(ref[:, columns:].astype(F32), axis=1, keepdims=True)
        if finish:
            sums = (sums * lax.rsqrt(norm / model + NORM_EPS)).astype(BF16)
            for head in range(columns // (2 * width)):
                for kind, out_ref in enumerate(out_refs):
                    start = (2 * head + kind) * width
                    out_ref[rows, head * width : (head + 1) * width] = sums[:, start : start + width]
        else:
            high = norm.astype(BF16).astype(F32)
            middle = (norm - high).astype(BF16).astype(F32)
            low = norm - high - middle
            lane = lax.broadcasted_iota(jnp.int32, (tokens, width), 1)
            lanes = jnp.where(lane == 0, high, jnp.where(lane == 1, middle, 0.0))
            out_refs[i][:, :columns] = sums.astype(BF16)
            out_refs[i][:, columns:] = jnp.where(lane == 2, low, lanes).astype(BF16)


def cache_projection(own, other, weights, width, model, added=(), finish=False, after=()):
    tokens, columns = own.shape[0], weights[0].shape[1]
    out = (tokens, columns // 2) if finish else (tokens // 2, columns + width)
    return resident_call(
        "cache_projection",
        functools.partial(cache_kernel, width, model, [half for _, half in added], finish),
        (own, other, *weights, *[array for array, _ in added]),
        [jax.ShapeDtypeStruct(out, BF16)] * 2,
        after=after,
    )


SIZES = (4, 2, 2, 2)
DEVICES = math.prod(SIZES)
DEPTH = SIZES[0]
PLACES = DEVICES // DEPTH


def swap(array, distance):
    return lax.ppermute(array, SEQ, [(i, i ^ distance) for i in range(DEVICES)])


def hop(array, steps):
    pairs = [
        (a * PLACES + i, b * PLACES + i) for a, b in sorted(steps.items()) for i in range(PLACES)
    ]
    return lax.ppermute(array, SEQ, pairs)


def shared_on_device(
    queries, keys, values, gate, residual, log_decay, out_weight, norm_gain, kv_weight
):
    tokens, heads = log_decay.shape
    width = queries.shape[1] // heads
    model = out_weight.shape[1]
    share = model // PLACES
    piece = share // DEPTH
    core = lax.axis_index("c")
    place = 4 * lax.axis_index("y") + 2 * lax.axis_index("x") + core

    with jax.named_scope("kv_weight_gather"):
        kv_mine = lax.all_gather(kv_weight, "z", axis=0, tiled=True)
    running = jnp.cumsum(log_decay, axis=0)
    per = heads // PLACES
    within = running.reshape(tokens, PLACES, per).transpose(1, 0, 2)
    across = running.T.reshape(PLACES, per, tokens)
    states = local_states(keys, values, log_decay, PLACES, width)
    with jax.named_scope("state_scan"):
        parts = lax.all_to_all(states, PLANE, 0, 0, tiled=True)

    even, odd = deal((residual, out_weight), place, PLACES, piece, after=(states,))
    starts, weights = pair(even, swap(odd, 1), (tokens, out_weight.shape[0]))
    with jax.named_scope("out_weight_gather"):
        weights = [swap(part, 2 * chip) if chip else part for chip, part in enumerate(weights)]
    with jax.named_scope("residual_exchange"):
        starts = [starts[0], swap(starts[1], 2), swap(starts[2], 4), starts[3]]
    with jax.named_scope("state_scan"):
        total = plane_total(parts, per, width, after=(starts[0],))
        nearest = hop(total, {a: a + 1 for a in range(DEPTH - 1)})
        joined = join(nearest, total, width)
        others = hop(joined, {a: a + 2 for a in range(DEPTH - 2)})
    with jax.named_scope("out_weight_gather"):
        shard = in_order(weights, place, after=(total,))
        out_full = lax.all_gather(*hold((shard,), (kv_mine,)), "z", axis=0, tiled=True)
    with jax.named_scope("state_scan"):
        prefix = plane_prefix(
            parts, nearest, others, width, after=(kv_mine, shard, starts[1], starts[2])
        )
        entering = lax.all_to_all(prefix, PLANE, 0, 0, tiled=True)
        entering = entering.reshape(heads, width, width)
    intra, opened = local_intra(
        queries, keys, values, gate, within, across, width, after=(prefix,)
    )
    with jax.named_scope("residual_exchange"):
        (starts[3],) = hold((starts[3],), (prefix,))
        starts[3] = swap(starts[3], 6)

    early, late = mix(queries, opened, intra, within, entering, width)
    early, late = hold((early, late), (starts[3],))

    with jax.named_scope("cache_weight"):
        gains = norm_gain.reshape(DEPTH, PLACES, piece)
        kv_full = []
        for r, rows in enumerate((kv_mine, swap(kv_mine, 1))):
            gain = lax.dynamic_index_in_dim(gains, place ^ r, 1, False).reshape(share, 1)
            kv_full.append((rows.astype(F32) * gain.astype(F32)).astype(BF16))

    def hidden_of(*halves, after=()):
        pieces = [(half, (mixed, swap(mixed, 1)), starts[chip]) for chip, half, mixed in halves]
        mine, theirs = out_projection(pieces, out_full, after)
        return mine, swap(theirs, 1)

    def share_of(hidden, added=(), finish=False, after=()):
        return cache_projection(*hidden, kv_full, width, model, added, finish, after)

    with jax.named_scope("projections"):
        early_x, late_y = swap(early, 2), swap(late, 4)
        early_far, late_far = swap(early_x, 4), swap(late_y, 2)
        near = hidden_of((1, 0, early_x), (2, 1, late_y))
        early, late = hold((early, late), (early_far, late_far))
        late_x, early_y = swap(late, 2), swap(early, 4)
        far = hidden_of((3, 0, early_far), (3, 1, late_far), after=(near[0],))
        early_far, late_far = share_of(far)
        early_x, late_y = share_of(near, after=(early_far,))
        late_x, early_y = hold((late_x, early_y), (early_x,))
        early_x, late_y = swap(early_x, 2), swap(late_y, 4)
        late_far, early_far = swap(late_far, 4), swap(early_far, 2)
        near = hidden_of((1, 1, late_x), (2, 0, early_y))
        late_x, early_y = share_of(near, [(late_far, 0), (early_far, 1)])
        home = hidden_of((0, 0, early), (0, 1, late), after=(late_x, early_x, late_y))
        late_x, early_y = swap(late_x, 2), swap(early_y, 4)
        added = [(early_x, 0), (late_x, 1), (early_y, 0), (late_y, 1)]
        return share_of(home, added, True)


def entering(part, axis, combine, identity):
    place = lax.axis_index(axis)
    gathered = jax.tree.map(lambda a: lax.all_gather(a, axis), part)
    state = jax.tree.map(lambda a, e: jnp.zeros_like(a) + jnp.asarray(e, a.dtype), part, identity)

    def one(step, state):
        return combine(
            state, jax.tree.map(lambda a: lax.dynamic_index_in_dim(a, step, 0, False), gathered)
        )

    return lax.fori_loop(0, place, one, state)


def local_retention(queries, keys, values, log_decay, block):
    tokens, heads, width = queries.shape
    count = tokens // block

    def to_blocks(array):
        return array.reshape((count, block) + array.shape[1:])

    lower = jnp.arange(block)[:, None] >= jnp.arange(block)[None, :]

    def advance(carry, inputs):
        state, offset = carry
        query_block, key_block, value_block, decay_block = inputs
        within = jnp.cumsum(decay_block, axis=0)
        spread = within[:, None, :] - within[None, :, :]
        factor = jnp.where(
            lower[:, :, None], jnp.exp(jnp.where(lower[:, :, None], spread, 0.0)), 0.0
        )
        scores = jnp.einsum(
            "ihd,jhd->hij", query_block, key_block, preferred_element_type=jnp.float32
        )
        weighted = scores * jnp.transpose(factor, (2, 0, 1))
        values_wide = value_block.astype(jnp.float32)
        intra = jnp.einsum("hij,jhd->ihd", weighted, values_wide, precision=HIGHEST)
        query_wide = query_block.astype(jnp.float32)
        carried = jnp.exp(within)[:, :, None] * jnp.einsum(
            "ihd,hde->ihe", query_wide, state, precision=HIGHEST
        )
        ending = within[-1]
        key_wide = key_block.astype(jnp.float32) * jnp.exp(ending[None, :] - within)[:, :, None]
        fresh = jnp.exp(ending)[:, None, None] * state + jnp.einsum(
            "jhd,jhe->hde", key_wide, values_wide, precision=HIGHEST
        )
        return ((fresh, offset + ending), (intra + carried, offset[None, :] + within))

    start = (jnp.zeros((heads, width, width), jnp.float32), jnp.zeros((heads,), jnp.float32))
    final, stacked = lax.scan(
        advance,
        start,
        (to_blocks(queries), to_blocks(keys), to_blocks(values), to_blocks(log_decay)),
    )
    return (
        stacked[0].reshape(tokens, heads, width),
        stacked[1].reshape(tokens, heads),
        final[0],
        final[1],
    )


def combine_states(earlier, later):
    return (earlier[0] * later[0], later[0][:, None, None] * earlier[1] + later[1])


def on_device(queries, keys, values, gate, residual, log_decay, out_weight, norm_gain, kv_weight):
    tokens = queries.shape[0]
    heads = log_decay.shape[1]
    width = queries.shape[1] // heads
    shaped = [array.reshape(tokens, heads, width) for array in (queries, keys, values)]
    partial_out, running, state, offset = local_retention(
        shaped[0], shaped[1], shaped[2], log_decay, min(512, tokens)
    )
    identity = (jnp.ones((heads,), jnp.float32), jnp.zeros((heads, width, width), jnp.float32))
    scan_decay, incoming = entering((jnp.exp(offset), state), "seq", combine_states, identity)
    retained = partial_out + jnp.exp(running)[:, :, None] * jnp.einsum(
        "thd,hde->the", shaped[0].astype(jnp.float32), incoming, precision=HIGHEST
    )
    scale = lax.rsqrt(jnp.mean(retained * retained, axis=2, keepdims=True) + 1e-06)
    mixed = (
        jax.nn.silu(gate.astype(jnp.float32)) * (retained * scale).reshape(tokens, heads * width)
    ).astype(jnp.bfloat16)
    all_heads = lax.all_gather(mixed, "head", axis=1, tiled=True)
    out_full, kv_full = (
        lax.all_gather(out_weight, "seq", axis=0, tiled=True),
        lax.all_gather(kv_weight, "seq", axis=0, tiled=True),
    )
    branch = jnp.dot(all_heads, out_full, preferred_element_type=jnp.float32)
    hidden = (residual.astype(jnp.float32) + branch).astype(jnp.bfloat16)
    wide = hidden.astype(jnp.float32)
    squares = lax.psum(jnp.sum(wide * wide, axis=1), "head")
    features = wide.shape[1] * lax.axis_size("head")
    inverse = lax.rsqrt(squares[:, None] / features + 1e-06)
    local_norm = (wide * inverse * norm_gain.astype(jnp.float32)[None, :]).astype(jnp.bfloat16)
    normalized = lax.all_gather(local_norm, "head", axis=1, tiled=True)
    projected = jnp.dot(normalized, kv_full, preferred_element_type=jnp.float32)
    cache_heads = kv_weight.shape[1] // (2 * width)
    arranged = projected.reshape(tokens, cache_heads, 2, width)
    cache_keys = arranged[:, :, 0, :].reshape(tokens, cache_heads * width).astype(jnp.bfloat16)
    cache_values = arranged[:, :, 1, :].reshape(tokens, cache_heads * width).astype(jnp.bfloat16)
    return (cache_keys, cache_values)


def solution(mesh):
    devices, split = mesh.shape["seq"], mesh.shape["head"]
    if split == 1 and devices == DEVICES:
        fine = Mesh(mesh.devices.reshape(SIZES + (1,)), SEQ + ("head",))
        placed, copied = P(SEQ, "head"), P("head")
        return jax.shard_map(
            shared_on_device,
            mesh=fine,
            in_specs=(placed,) * 7 + (copied, placed),
            out_specs=(placed, placed),
            check_vma=False,
        )
    placed = P("seq", "head")
    return jax.shard_map(
        on_device,
        mesh=mesh,
        in_specs=(placed,) * 7 + (P("head"), placed),
        out_specs=(placed, placed),
        check_vma=False,
    )
```

```python
import functools
import math

import jax
import jax.numpy as jnp
from jax import lax
from jax.experimental import pallas as pl
from jax.experimental.pallas import tpu as pltpu
from jax.sharding import Mesh
from jax.sharding import PartitionSpec as P

F32, BF16 = jnp.float32, jnp.bfloat16
HIGHEST = lax.Precision.HIGHEST
NORM_EPS = 1e-06
DECAY_ROWS = 16
PLANE = ("y", "x", "c")
SEQ = ("z", "y", "x", "c")
MIB = 1024 * 1024
VMEM_STREAMED = {"local_states": 60 * MIB, "local_intra": 54 * MIB, "mix": 60 * MIB}
VMEM_RESIDENT = 16 * MIB


def split_rows(total):
    high = total.astype(BF16).astype(F32)
    middle = (total - high).astype(BF16).astype(F32)
    low = total - high - middle
    row = lax.broadcasted_iota(jnp.int32, (DECAY_ROWS, total.shape[1]), 0)
    rows = jnp.where(row == 0, high, jnp.where(row == 1, middle, jnp.where(row == 2, low, 0.0)))
    return rows.astype(BF16)


def join_rows(rows):
    return jnp.sum(rows.astype(F32), axis=0, keepdims=True)


def dot(a, b, contract):
    return lax.dot_general(a, b, (contract, ((), ())), preferred_element_type=F32)


def state_kernel(width, key_ref, value_ref, decay_ref, out_ref, fade_ref, ending_ref):
    tokens = key_ref.shape[0]
    groups, _, per = fade_ref.shape

    @pl.when(pl.program_id(0) == 0)
    def _():
        decay = decay_ref[...]
        later = lax.broadcasted_iota(jnp.int32, (tokens, tokens), 0) < lax.broadcasted_iota(
            jnp.int32, (tokens, tokens), 1
        )
        rest = lax.dot_general(
            later.astype(F32),
            decay,
            (((1,), (1,)), ((), ())),
            precision=HIGHEST,
            preferred_element_type=F32,
        )
        fade = jnp.exp(rest)
        ending = rest[:1] + jnp.transpose(decay)[:1]
        for i in range(groups):
            fade_ref[i] = fade[:, i * per : (i + 1) * per]
            ending_ref[i] = ending[:, i * per : (i + 1) * per]

    rows = width + DECAY_ROWS
    for i in range(out_ref.shape[0]):
        place = pl.program_id(0) * out_ref.shape[0] + i
        fade, ending = fade_ref[place], ending_ref[place]
        for head in range(per):
            columns = slice((i * per + head) * width, (i * per + head + 1) * width)
            faded = (key_ref[:, columns].astype(F32) * fade[:, head : head + 1]).astype(BF16)
            state = dot(faded, value_ref[:, columns], ((0,), (0,)))
            out_ref[i, head * rows : head * rows + width, :] = state.astype(BF16)
            total = jnp.broadcast_to(ending[:, head : head + 1], (1, width))
            out_ref[i, head * rows + width : (head + 1) * rows, :] = split_rows(total)


def intra_kernel(
    width, query_ref, key_ref, value_ref, gate_ref, within_ref, across_ref, out_ref, open_ref
):
    tokens = query_ref.shape[0]
    within, across = within_ref[0], across_ref[0]
    lower = lax.broadcasted_iota(jnp.int32, (tokens, tokens), 0) >= lax.broadcasted_iota(
        jnp.int32, (tokens, tokens), 1
    )
    for head in range(within.shape[1]):
        columns = slice(head * width, (head + 1) * width)
        scores = dot(query_ref[:, columns], key_ref[:, columns], ((1,), (1,)))
        spread = within[:, head : head + 1] - across[head : head + 1, :]
        weighted = jnp.where(lower, scores * jnp.exp(jnp.where(lower, spread, 0.0)), 0.0)
        local = dot(weighted.astype(BF16), value_ref[:, columns], ((1,), (0,)))
        out_ref[:, columns] = local.astype(BF16)
        gate = gate_ref[:, columns].astype(F32)
        open_ref[:, columns] = (gate / (1.0 + jnp.exp(-gate))).astype(BF16)


def mix_kernel(width, query_ref, open_ref, intra_ref, within_ref, state_ref, *out_refs):
    rows = out_refs[0].shape[0]
    groups, _, per = within_ref.shape
    for head in range(groups * per):
        reach = jnp.exp(within_ref[head // per])[:, head % per : head % per + 1]
        columns = slice(head * width, (head + 1) * width)
        carried = dot(query_ref[:, columns], state_ref[head], ((1,), (0,)))
        retained = intra_ref[:, columns].astype(F32) + reach * carried
        scale = lax.rsqrt(jnp.mean(retained * retained, axis=1, keepdims=True) + NORM_EPS)
        mixed = (open_ref[:, columns].astype(F32) * (retained * scale)).astype(BF16)
        for half, out_ref in enumerate(out_refs):
            out_ref[:, columns] = mixed[half * rows : (half + 1) * rows]


def total_kernel(width, parts_ref, out_ref):
    for head in range(out_ref.shape[0]):
        top = head * (width + DECAY_ROWS)
        states, decays = slice(top, top + width), slice(top + width, top + width + DECAY_ROWS)
        state = jnp.zeros((width, width), F32)
        total = jnp.zeros((1, width), F32)
        for place in range(parts_ref.shape[0]):
            ending = join_rows(parts_ref[place, decays, :])
            state = jnp.exp(ending) * state + parts_ref[place, states, :].astype(F32)
            total = total + ending
        out_ref[head, :width, :] = state.astype(BF16)
        out_ref[head, width:, :] = split_rows(total)


def join_kernel(width, earlier_ref, later_ref, out_ref):
    for head in range(out_ref.shape[0]):
        ending = join_rows(later_ref[head, width:, :])
        state = jnp.exp(ending) * earlier_ref[head, :width, :].astype(F32)
        out_ref[head, :width, :] = (state + later_ref[head, :width, :].astype(F32)).astype(BF16)
        out_ref[head, width:, :] = split_rows(join_rows(earlier_ref[head, width:, :]) + ending)


def prefix_kernel(width, parts_ref, nearest_ref, others_ref, out_ref):
    for head in range(nearest_ref.shape[0]):
        top = head * (width + DECAY_ROWS)
        states, decays = slice(top, top + width), slice(top + width, top + width + DECAY_ROWS)
        reach = jnp.exp(join_rows(nearest_ref[head, width:, :]))
        state = reach * others_ref[head, :width, :].astype(F32)
        state = state + nearest_ref[head, :width, :].astype(F32)
        for place in range(parts_ref.shape[0]):
            out_ref[place, head] = state.astype(BF16)
            ending = join_rows(parts_ref[place, decays, :])
            state = jnp.exp(ending) * state + parts_ref[place, states, :].astype(F32)


def local_call(
    name, body, grid, operands, specs, out_specs, out_shape, scalars=(), scratch=(), after=()
):
    taken = len(scalars) + len(operands)

    def kernel(*refs):
        body(*refs[:taken], *refs[taken + len(after) :])

    return pl.pallas_call(
        kernel,
        grid_spec=pltpu.PrefetchScalarGridSpec(
            num_scalar_prefetch=len(scalars),
            grid=(grid,),
            in_specs=list(specs) + [pl.BlockSpec(memory_space=pltpu.HBM)] * len(after),
            out_specs=out_specs,
            scratch_shapes=scratch,
        ),
        out_shape=out_shape,
        compiler_params=pltpu.CompilerParams(vmem_limit_bytes=VMEM_STREAMED[name]),
        name=name,
    )(*scalars, *operands, *after)


def resident(count):
    return [pl.BlockSpec(memory_space=pltpu.VMEM)] * count


def resident_call(name, body, operands, out_shape, scalars=(), after=()):
    taken = len(scalars) + len(operands)

    def kernel(*refs):
        body(*refs[:taken], *refs[taken + len(after) :])

    return pl.pallas_call(
        kernel,
        in_specs=[pl.BlockSpec(memory_space=pltpu.SMEM)] * len(scalars)
        + resident(len(operands))
        + [pl.BlockSpec(memory_space=pltpu.HBM)] * len(after),
        out_specs=resident(len(out_shape)),
        out_shape=out_shape,
        compiler_params=pltpu.CompilerParams(vmem_limit_bytes=VMEM_RESIDENT),
        name=name,
    )(*scalars, *operands, *after)


def wide(rows, columns):
    return pl.BlockSpec((rows, columns), lambda i, *_: (0, i))


def whole(rows, columns):
    return pl.BlockSpec((rows, columns), lambda i, *_: (0, 0))


def group(*shape):
    return pl.BlockSpec((1,) + shape, lambda i, *_: (i, 0, 0))


def local_states(keys, values, decays, groups, width, after=()):
    heads, tokens = decays.shape
    per, steps = heads // groups, groups // 2
    tall = per * (width + DECAY_ROWS)
    wider = wide(tokens, 2 * per * width)
    return local_call(
        "local_states",
        functools.partial(state_kernel, width),
        steps,
        (keys, values, decays),
        (wider, wider, whole(heads, tokens)),
        pl.BlockSpec((2, tall, width), lambda i: (i, 0, 0)),
        jax.ShapeDtypeStruct((groups, tall, width), BF16),
        scratch=(pltpu.VMEM((groups, tokens, per), F32), pltpu.VMEM((groups, 1, per), F32)),
        after=after,
    )


def local_intra(queries, keys, values, gate, within, across, width, after=()):
    tokens, groups, per = keys.shape[0], within.shape[0], within.shape[2]
    heads = wide(tokens, per * width)
    return local_call(
        "local_intra",
        functools.partial(intra_kernel, width),
        groups,
        (queries, keys, values, gate, within, across),
        (heads, heads, heads, heads, group(tokens, per), group(per, tokens)),
        [heads, heads],
        [jax.ShapeDtypeStruct(queries.shape, BF16)] * 2,
        after=after,
    )


def mix(queries, opened, intra, within, states, width, after=()):
    groups, tokens, per = within.shape
    heads = 2 * per
    wider = wide(tokens, heads * width)
    return local_call(
        "mix",
        functools.partial(mix_kernel, width),
        groups // 2,
        (queries, opened, intra, within, states),
        (
            wider,
            wider,
            wider,
            pl.BlockSpec((2, tokens, per), lambda i: (i, 0, 0)),
            pl.BlockSpec((heads, width, width), lambda i: (i, 0, 0)),
        ),
        [wide(tokens // 2, heads * width)] * 2,
        [jax.ShapeDtypeStruct((tokens // 2, queries.shape[1]), BF16)] * 2,
        after=after,
    )


def plane_total(parts, heads, width, after=()):
    shape = jax.ShapeDtypeStruct((heads, width + DECAY_ROWS, width), BF16)
    body = functools.partial(total_kernel, width)
    return resident_call("plane_total", body, (parts,), [shape], after=after)[0]


def join(earlier, later, width, after=()):
    shape = jax.ShapeDtypeStruct(later.shape, BF16)
    body = functools.partial(join_kernel, width)
    return resident_call("join", body, (earlier, later), [shape], after=after)[0]


def plane_prefix(parts, nearest, others, width, after=()):
    shape = jax.ShapeDtypeStruct((parts.shape[0], nearest.shape[0], width, width), BF16)
    body = functools.partial(prefix_kernel, width)
    return resident_call("plane_prefix", body, (parts, nearest, others), [shape], after=after)[0]


def deal_kernel(ways, block, place_ref, *refs):
    *source_refs, even_ref, odd_ref = refs
    for r in range(ways):
        target_ref, top = (even_ref, odd_ref)[r % 2], 0
        for source_ref in source_refs:
            rows = slice(top, top + source_ref.shape[0])
            for i in range(target_ref.shape[2] // block):
                start = pl.multiple_of((i * ways + (place_ref[0] ^ r)) * block, block)
                columns = slice(i * block, (i + 1) * block)
                target_ref[r // 2, rows, columns] = source_ref[:, pl.ds(start, block)]
            top += source_ref.shape[0]


def deal(arrays, place, ways, block, after=()):
    rows = sum(array.shape[0] for array in arrays)
    shape = jax.ShapeDtypeStruct((ways // 2, rows, arrays[0].shape[1] // ways), BF16)
    return resident_call(
        "deal",
        functools.partial(deal_kernel, ways, block),
        arrays,
        [shape, shape],
        scalars=(place.reshape(1),),
        after=after,
    )


def pair_kernel(parts, even_ref, odd_ref, *target_refs):
    for (chip, top), target_ref in zip(parts, target_refs):
        rows = slice(top, top + target_ref.shape[1])
        target_ref[0] = even_ref[chip, rows, :]
        target_ref[1] = odd_ref[chip, rows, :]


def pair(even, odd, split, after=()):
    chips, rows, columns = even.shape
    parts = [(chip, 0) for chip in range(chips)] + [(chips - 1, split)]
    heights = [rows] * (chips - 1) + [split, rows - split]
    return resident_call(
        "pair",
        functools.partial(pair_kernel, parts),
        (even, odd),
        [jax.ShapeDtypeStruct((2, height, columns), even.dtype) for height in heights],
        after=after,
    )


def order_kernel(place_ref, *refs):
    *sources, target_ref = refs
    rows = sources[-1].shape[1]
    for r in range(2 * len(sources)):
        source = sources[r // 2]
        start = pl.multiple_of((place_ref[0] ^ r) * rows, rows)
        target_ref[pl.ds(start, rows), :] = source[r % 2, source.shape[1] - rows :, :]


def in_order(arrays, place, after=()):
    _, rows, columns = arrays[-1].shape
    tall = (2 * len(arrays) * rows, columns)
    return resident_call(
        "in_order",
        order_kernel,
        arrays,
        [jax.ShapeDtypeStruct(tall, arrays[0].dtype)],
        scalars=(place.reshape(1),),
        after=after,
    )[0]


def hold(arrays, after):
    kept, count = pl.BlockSpec(memory_space=pltpu.HBM), len(arrays)
    return pl.pallas_call(
        lambda *refs: None,
        in_specs=[kept] * (count + len(after)),
        out_specs=[kept] * count,
        out_shape=[jax.ShapeDtypeStruct(array.shape, array.dtype) for array in arrays],
        input_output_aliases={i: i for i in range(count)},
        compiler_params=pltpu.CompilerParams(vmem_limit_bytes=VMEM_RESIDENT),
        name="hold",
    )(*arrays, *after)


def out_kernel(halves, *refs):
    chips, pieces = len(halves), 2 * len(halves)
    mixed, weight_ref, start_refs = refs[:pieces], refs[pieces], refs[pieces + 1 : -2]
    tokens, depth = mixed[0].shape
    step = min(depth, 512)
    total = jnp.zeros((pieces * tokens, weight_ref.shape[1]), F32)
    for start in range(0, depth, step):
        left = jnp.concatenate([ref[:, start : start + step] for ref in mixed], axis=0)
        total = total + dot(left, weight_ref[start : start + step, :], ((1,), (0,)))
    for chip in range(chips):
        rows = slice(halves[chip] * tokens, (halves[chip] + 1) * tokens)
        for core, out_ref in enumerate(refs[-2:]):
            i = 2 * chip + core
            hidden = start_refs[chip][core, rows, :].astype(F32)
            hidden = hidden + total[i * tokens : (i + 1) * tokens]
            out_ref[chip * tokens : (chip + 1) * tokens, :] = hidden.astype(BF16)


def out_projection(pieces, weight, after=()):
    halves, mixed, starts = zip(*pieces)
    mixed = [array for cores in mixed for array in cores]
    shape = jax.ShapeDtypeStruct((len(pieces) * mixed[0].shape[0], weight.shape[1]), BF16)
    return resident_call(
        "out_projection",
        functools.partial(out_kernel, halves),
        (*mixed, weight, *starts),
        [shape, shape],
        after=after,
    )


def cache_kernel(width, model, joined, finish, *refs):
    own_ref, other_ref, own_weight_ref, other_weight_ref, *refs = refs
    added, out_refs = refs[: len(joined)], refs[len(joined) :]
    tokens, columns = own_ref.shape[0] // 2, own_weight_ref.shape[1]
    own, other = own_ref[...], other_ref[...]
    total = dot(own, own_weight_ref[...], ((1,), (0,)))
    total = total + dot(other, other_weight_ref[...], ((1,), (0,)))
    squares = jnp.square(own.astype(F32)) + jnp.square(other.astype(F32))
    squares = jnp.sum(squares, axis=1, keepdims=True)
    for i in range(2):
        rows = slice(i * tokens, (i + 1) * tokens)
        sums, norm = total[rows], squares[rows]
        for ref, half in zip(added, joined):
            if half == i:
                sums = sums + ref[:, :columns].astype(F32)
                norm = norm + jnp.sum(ref[:, columns:].astype(F32), axis=1, keepdims=True)
        if finish:
            sums = (sums * lax.rsqrt(norm / model + NORM_EPS)).astype(BF16)
            for head in range(columns // (2 * width)):
                for kind, out_ref in enumerate(out_refs):
                    start = (2 * head + kind) * width
                    out_ref[rows, head * width : (head + 1) * width] = sums[:, start : start + width]
        else:
            high = norm.astype(BF16).astype(F32)
            middle = (norm - high).astype(BF16).astype(F32)
            low = norm - high - middle
            lane = lax.broadcasted_iota(jnp.int32, (tokens, width), 1)
            lanes = jnp.where(lane == 0, high, jnp.where(lane == 1, middle, 0.0))
            out_refs[i][:, :columns] = sums.astype(BF16)
            out_refs[i][:, columns:] = jnp.where(lane == 2, low, lanes).astype(BF16)


def cache_projection(own, other, weights, width, model, added=(), finish=False, after=()):
    tokens, columns = own.shape[0], weights[0].shape[1]
    out = (tokens, columns // 2) if finish else (tokens // 2, columns + width)
    return resident_call(
        "cache_projection",
        functools.partial(cache_kernel, width, model, [half for _, half in added], finish),
        (own, other, *weights, *[array for array, _ in added]),
        [jax.ShapeDtypeStruct(out, BF16)] * 2,
        after=after,
    )


SIZES = (4, 2, 2, 2)
DEVICES = math.prod(SIZES)
DEPTH = SIZES[0]
PLACES = DEVICES // DEPTH


def swap(array, distance):
    return lax.ppermute(array, SEQ, [(i, i ^ distance) for i in range(DEVICES)])


def hop(array, steps):
    pairs = [
        (a * PLACES + i, b * PLACES + i) for a, b in sorted(steps.items()) for i in range(PLACES)
    ]
    return lax.ppermute(array, SEQ, pairs)


def shared_on_device(
    queries, keys, values, gate, residual, log_decay, out_weight, norm_gain, kv_weight
):
    tokens, heads = log_decay.shape
    width = queries.shape[1] // heads
    model = out_weight.shape[1]
    share = model // PLACES
    piece = share // DEPTH
    core = lax.axis_index("c")
    place = 4 * lax.axis_index("y") + 2 * lax.axis_index("x") + core

    with jax.named_scope("kv_weight_gather"):
        kv_mine = lax.all_gather(kv_weight, "z", axis=0, tiled=True)
    running = jnp.cumsum(log_decay, axis=0)
    per = heads // PLACES
    within = running.reshape(tokens, PLACES, per).transpose(1, 0, 2)
    across = running.T.reshape(PLACES, per, tokens)
    states = local_states(keys, values, log_decay.T, PLACES, width)
    with jax.named_scope("state_scan"):
        parts = lax.all_to_all(states, PLANE, 0, 0, tiled=True)

    even, odd = deal((residual, out_weight), place, PLACES, piece, after=(states,))
    with jax.named_scope("start_exchange"):
        *starts, far_weight = pair(even, swap(odd, 1), tokens)
        starts[1:3] = [swap(starts[1], 2), swap(starts[2], 4)]
        far_weight = swap(far_weight, 6)
    with jax.named_scope("state_scan"):
        total = plane_total(parts, per, width, after=(starts[0],))
        nearest = hop(total, {a: a + 1 for a in range(DEPTH - 1)})
        joined = join(nearest, total, width)
        others = hop(joined, {a: a + 2 for a in range(DEPTH - 2)})
    with jax.named_scope("out_weight_gather"):
        shard = in_order((*starts[:3], far_weight), place, after=(total,))
        out_full = lax.all_gather(*hold((shard,), (kv_mine,)), "z", axis=0, tiled=True)
    with jax.named_scope("state_scan"):
        prefix = plane_prefix(
            parts, nearest, others, width, after=(kv_mine, shard)
        )
        entering = lax.all_to_all(prefix, PLANE, 0, 0, tiled=True)
        entering = entering.reshape(heads, width, width)
    intra, opened = local_intra(
        queries, keys, values, gate, within, across, width, after=(prefix,)
    )
    with jax.named_scope("residual_exchange"):
        (starts[3],) = hold((starts[3],), (prefix,))
        starts[3] = swap(starts[3], 6)

    early, late = mix(queries, opened, intra, within, entering, width)
    early, late = hold((early, late), (starts[3],))

    with jax.named_scope("cache_weight"):
        gains = norm_gain.reshape(DEPTH, PLACES, piece)
        kv_full = []
        for r, rows in enumerate((kv_mine, swap(kv_mine, 1))):
            gain = lax.dynamic_index_in_dim(gains, place ^ r, 1, False).reshape(share, 1)
            kv_full.append((rows.astype(F32) * gain.astype(F32)).astype(BF16))

    def cores(mixed):
        return mixed, swap(mixed, 1)

    def hidden_of(*halves, after=()):
        pieces = [(half, mixed, starts[chip]) for chip, half, mixed in halves]
        mine, theirs = out_projection(pieces, out_full, after)
        return mine, swap(theirs, 1)

    def share_of(hidden, added=(), finish=False, after=()):
        return cache_projection(*hidden, kv_full, width, model, added, finish, after)

    with jax.named_scope("projections"):
        early_x, late_y = swap(early, 2), swap(late, 4)
        early_far, late_far = swap(early_x, 4), swap(late_y, 2)
        crossed = swap(early, 1), swap(late, 1)
        near = hidden_of(
            (1, 0, cores(early_x)), (2, 1, cores(late_y)), after=crossed
        )
        early, late = hold((early, late), (early_far, late_far))
        home = (0, 0, (early, crossed[0])), (0, 1, (late, crossed[1]))
        late_x, early_y = swap(late, 2), swap(early, 4)
        far = hidden_of((3, 0, cores(early_far)), (3, 1, cores(late_far)), after=(near[0],))
        early_far, late_far = share_of(far)
        early_x, late_y = share_of(near, after=(early_far,))
        late_x, early_y = hold((late_x, early_y), (early_x,))
        early_x, late_y = swap(early_x, 2), swap(late_y, 4)
        late_far, early_far = swap(late_far, 4), swap(early_far, 2)
        near = hidden_of((1, 1, cores(late_x)), (2, 0, cores(early_y)))
        late_x, early_y = share_of(near, [(late_far, 0), (early_far, 1)])
        home = hidden_of(*home, after=(late_x, early_x, late_y))
        late_x, early_y = swap(late_x, 2), swap(early_y, 4)
        added = [(early_x, 0), (late_x, 1), (early_y, 0), (late_y, 1)]
        return share_of(home, added, True)


def entering(part, axis, combine, identity):
    place = lax.axis_index(axis)
    gathered = jax.tree.map(lambda a: lax.all_gather(a, axis), part)
    state = jax.tree.map(lambda a, e: jnp.zeros_like(a) + jnp.asarray(e, a.dtype), part, identity)

    def one(step, state):
        return combine(
            state, jax.tree.map(lambda a: lax.dynamic_index_in_dim(a, step, 0, False), gathered)
        )

    return lax.fori_loop(0, place, one, state)


def local_retention(queries, keys, values, log_decay, block):
    tokens, heads, width = queries.shape
    count = tokens // block

    def to_blocks(array):
        return array.reshape((count, block) + array.shape[1:])

    lower = jnp.arange(block)[:, None] >= jnp.arange(block)[None, :]

    def advance(carry, inputs):
        state, offset = carry
        query_block, key_block, value_block, decay_block = inputs
        within = jnp.cumsum(decay_block, axis=0)
        spread = within[:, None, :] - within[None, :, :]
        factor = jnp.where(
            lower[:, :, None], jnp.exp(jnp.where(lower[:, :, None], spread, 0.0)), 0.0
        )
        scores = jnp.einsum(
            "ihd,jhd->hij", query_block, key_block, preferred_element_type=jnp.float32
        )
        weighted = scores * jnp.transpose(factor, (2, 0, 1))
        values_wide = value_block.astype(jnp.float32)
        intra = jnp.einsum("hij,jhd->ihd", weighted, values_wide, precision=HIGHEST)
        query_wide = query_block.astype(jnp.float32)
        carried = jnp.exp(within)[:, :, None] * jnp.einsum(
            "ihd,hde->ihe", query_wide, state, precision=HIGHEST
        )
        ending = within[-1]
        key_wide = key_block.astype(jnp.float32) * jnp.exp(ending[None, :] - within)[:, :, None]
        fresh = jnp.exp(ending)[:, None, None] * state + jnp.einsum(
            "jhd,jhe->hde", key_wide, values_wide, precision=HIGHEST
        )
        return ((fresh, offset + ending), (intra + carried, offset[None, :] + within))

    start = (jnp.zeros((heads, width, width), jnp.float32), jnp.zeros((heads,), jnp.float32))
    final, stacked = lax.scan(
        advance,
        start,
        (to_blocks(queries), to_blocks(keys), to_blocks(values), to_blocks(log_decay)),
    )
    return (
        stacked[0].reshape(tokens, heads, width),
        stacked[1].reshape(tokens, heads),
        final[0],
        final[1],
    )


def combine_states(earlier, later):
    return (earlier[0] * later[0], later[0][:, None, None] * earlier[1] + later[1])


def on_device(queries, keys, values, gate, residual, log_decay, out_weight, norm_gain, kv_weight):
    tokens = queries.shape[0]
    heads = log_decay.shape[1]
    width = queries.shape[1] // heads
    shaped = [array.reshape(tokens, heads, width) for array in (queries, keys, values)]
    partial_out, running, state, offset = local_retention(
        shaped[0], shaped[1], shaped[2], log_decay, min(512, tokens)
    )
    identity = (jnp.ones((heads,), jnp.float32), jnp.zeros((heads, width, width), jnp.float32))
    scan_decay, incoming = entering((jnp.exp(offset), state), "seq", combine_states, identity)
    retained = partial_out + jnp.exp(running)[:, :, None] * jnp.einsum(
        "thd,hde->the", shaped[0].astype(jnp.float32), incoming, precision=HIGHEST
    )
    scale = lax.rsqrt(jnp.mean(retained * retained, axis=2, keepdims=True) + 1e-06)
    mixed = (
        jax.nn.silu(gate.astype(jnp.float32)) * (retained * scale).reshape(tokens, heads * width)
    ).astype(jnp.bfloat16)
    all_heads = lax.all_gather(mixed, "head", axis=1, tiled=True)
    out_full, kv_full = (
        lax.all_gather(out_weight, "seq", axis=0, tiled=True),
        lax.all_gather(kv_weight, "seq", axis=0, tiled=True),
    )
    branch = jnp.dot(all_heads, out_full, preferred_element_type=jnp.float32)
    hidden = (residual.astype(jnp.float32) + branch).astype(jnp.bfloat16)
    wide = hidden.astype(jnp.float32)
    squares = lax.psum(jnp.sum(wide * wide, axis=1), "head")
    features = wide.shape[1] * lax.axis_size("head")
    inverse = lax.rsqrt(squares[:, None] / features + 1e-06)
    local_norm = (wide * inverse * norm_gain.astype(jnp.float32)[None, :]).astype(jnp.bfloat16)
    normalized = lax.all_gather(local_norm, "head", axis=1, tiled=True)
    projected = jnp.dot(normalized, kv_full, preferred_element_type=jnp.float32)
    cache_heads = kv_weight.shape[1] // (2 * width)
    arranged = projected.reshape(tokens, cache_heads, 2, width)
    cache_keys = arranged[:, :, 0, :].reshape(tokens, cache_heads * width).astype(jnp.bfloat16)
    cache_values = arranged[:, :, 1, :].reshape(tokens, cache_heads * width).astype(jnp.bfloat16)
    return (cache_keys, cache_values)


def solution(mesh):
    devices, split = mesh.shape["seq"], mesh.shape["head"]
    if split == 1 and devices == DEVICES:
        fine = Mesh(mesh.devices.reshape(SIZES + (1,)), SEQ + ("head",))
        placed, copied = P(SEQ, "head"), P("head")
        return jax.shard_map(
            shared_on_device,
            mesh=fine,
            in_specs=(placed,) * 7 + (copied, placed),
            out_specs=(placed, placed),
            check_vma=False,
        )
    placed = P("seq", "head")
    return jax.shard_map(
        on_device,
        mesh=mesh,
        in_specs=(placed,) * 7 + (P("head"), placed),
        out_specs=(placed, placed),
        check_vma=False,
    )
```

```python
import functools
import math

import jax
import jax.numpy as jnp
from jax import lax
from jax.experimental import pallas as pl
from jax.experimental.pallas import tpu as pltpu
from jax.sharding import Mesh
from jax.sharding import PartitionSpec as P

F32, BF16 = jnp.float32, jnp.bfloat16
HIGHEST = lax.Precision.HIGHEST
NORM_EPS = 1e-06
DECAY_ROWS = 16
PLANE = ("y", "x", "c")
SEQ = ("z", "y", "x", "c")
MIB = 1024 * 1024
VMEM_STREAMED = {"local_states": 60 * MIB, "local_intra": 54 * MIB, "mix": 60 * MIB}
VMEM_RESIDENT = 16 * MIB


def split_rows(total):
    high = total.astype(BF16).astype(F32)
    middle = (total - high).astype(BF16).astype(F32)
    low = total - high - middle
    row = lax.broadcasted_iota(jnp.int32, (DECAY_ROWS, total.shape[1]), 0)
    rows = jnp.where(row == 0, high, jnp.where(row == 1, middle, jnp.where(row == 2, low, 0.0)))
    return rows.astype(BF16)


def join_rows(rows):
    return jnp.sum(rows.astype(F32), axis=0, keepdims=True)


def dot(a, b, contract):
    return lax.dot_general(a, b, (contract, ((), ())), preferred_element_type=F32)


def state_kernel(width, key_ref, value_ref, decay_ref, out_ref, fade_ref, ending_ref):
    tokens = key_ref.shape[0]
    groups, _, per = fade_ref.shape

    @pl.when(pl.program_id(0) == 0)
    def _():
        decay = decay_ref[...]
        later = lax.broadcasted_iota(jnp.int32, (tokens, tokens), 0) < lax.broadcasted_iota(
            jnp.int32, (tokens, tokens), 1
        )
        rest = lax.dot_general(
            later.astype(F32),
            decay,
            (((1,), (1,)), ((), ())),
            precision=HIGHEST,
            preferred_element_type=F32,
        )
        fade = jnp.exp(rest)
        ending = rest[:1] + jnp.transpose(decay)[:1]
        for i in range(groups):
            fade_ref[i] = fade[:, i * per : (i + 1) * per]
            ending_ref[i] = ending[:, i * per : (i + 1) * per]

    rows = width + DECAY_ROWS
    for i in range(out_ref.shape[0]):
        place = pl.program_id(0) * out_ref.shape[0] + i
        fade, ending = fade_ref[place], ending_ref[place]
        for head in range(per):
            columns = slice((i * per + head) * width, (i * per + head + 1) * width)
            faded = (key_ref[:, columns].astype(F32) * fade[:, head : head + 1]).astype(BF16)
            state = dot(faded, value_ref[:, columns], ((0,), (0,)))
            out_ref[i, head * rows : head * rows + width, :] = state.astype(BF16)
            total = jnp.broadcast_to(ending[:, head : head + 1], (1, width))
            out_ref[i, head * rows + width : (head + 1) * rows, :] = split_rows(total)


def intra_kernel(
    width, query_ref, key_ref, value_ref, gate_ref, within_ref, across_ref, out_ref, open_ref
):
    tokens = query_ref.shape[0]
    within, across = within_ref[0], across_ref[0]
    lower = lax.broadcasted_iota(jnp.int32, (tokens, tokens), 0) >= lax.broadcasted_iota(
        jnp.int32, (tokens, tokens), 1
    )
    for head in range(within.shape[1]):
        columns = slice(head * width, (head + 1) * width)
        scores = dot(query_ref[:, columns], key_ref[:, columns], ((1,), (1,)))
        spread = within[:, head : head + 1] - across[head : head + 1, :]
        weighted = jnp.where(lower, scores * jnp.exp(jnp.where(lower, spread, 0.0)), 0.0)
        local = dot(weighted.astype(BF16), value_ref[:, columns], ((1,), (0,)))
        out_ref[:, columns] = local.astype(BF16)
        gate = gate_ref[:, columns].astype(F32)
        open_ref[:, columns] = (gate / (1.0 + jnp.exp(-gate))).astype(BF16)


def mix_kernel(width, query_ref, open_ref, intra_ref, within_ref, state_ref, *out_refs):
    rows = out_refs[0].shape[0]
    groups, _, per = within_ref.shape
    for head in range(groups * per):
        reach = jnp.exp(within_ref[head // per])[:, head % per : head % per + 1]
        columns = slice(head * width, (head + 1) * width)
        carried = dot(query_ref[:, columns], state_ref[head], ((1,), (0,)))
        retained = intra_ref[:, columns].astype(F32) + reach * carried
        scale = lax.rsqrt(jnp.mean(retained * retained, axis=1, keepdims=True) + NORM_EPS)
        mixed = (open_ref[:, columns].astype(F32) * (retained * scale)).astype(BF16)
        for half, out_ref in enumerate(out_refs):
            out_ref[:, columns] = mixed[half * rows : (half + 1) * rows]


def total_kernel(width, parts_ref, out_ref):
    for head in range(out_ref.shape[0]):
        top = head * (width + DECAY_ROWS)
        states, decays = slice(top, top + width), slice(top + width, top + width + DECAY_ROWS)
        state = jnp.zeros((width, width), F32)
        total = jnp.zeros((1, width), F32)
        for place in range(parts_ref.shape[0]):
            ending = join_rows(parts_ref[place, decays, :])
            state = jnp.exp(ending) * state + parts_ref[place, states, :].astype(F32)
            total = total + ending
        out_ref[head, :width, :] = state.astype(BF16)
        out_ref[head, width:, :] = split_rows(total)


def join_kernel(width, earlier_ref, later_ref, out_ref):
    for head in range(out_ref.shape[0]):
        ending = join_rows(later_ref[head, width:, :])
        state = jnp.exp(ending) * earlier_ref[head, :width, :].astype(F32)
        out_ref[head, :width, :] = (state + later_ref[head, :width, :].astype(F32)).astype(BF16)
        out_ref[head, width:, :] = split_rows(join_rows(earlier_ref[head, width:, :]) + ending)


def prefix_kernel(width, parts_ref, nearest_ref, others_ref, out_ref):
    for head in range(nearest_ref.shape[0]):
        top = head * (width + DECAY_ROWS)
        states, decays = slice(top, top + width), slice(top + width, top + width + DECAY_ROWS)
        reach = jnp.exp(join_rows(nearest_ref[head, width:, :]))
        state = reach * others_ref[head, :width, :].astype(F32)
        state = state + nearest_ref[head, :width, :].astype(F32)
        for place in range(parts_ref.shape[0]):
            out_ref[place, head] = state.astype(BF16)
            ending = join_rows(parts_ref[place, decays, :])
            state = jnp.exp(ending) * state + parts_ref[place, states, :].astype(F32)


def local_call(
    name, body, grid, operands, specs, out_specs, out_shape, scalars=(), scratch=(), after=()
):
    taken = len(scalars) + len(operands)

    def kernel(*refs):
        body(*refs[:taken], *refs[taken + len(after) :])

    return pl.pallas_call(
        kernel,
        grid_spec=pltpu.PrefetchScalarGridSpec(
            num_scalar_prefetch=len(scalars),
            grid=(grid,),
            in_specs=list(specs) + [pl.BlockSpec(memory_space=pltpu.HBM)] * len(after),
            out_specs=out_specs,
            scratch_shapes=scratch,
        ),
        out_shape=out_shape,
        compiler_params=pltpu.CompilerParams(vmem_limit_bytes=VMEM_STREAMED[name]),
        name=name,
    )(*scalars, *operands, *after)


def resident(count):
    return [pl.BlockSpec(memory_space=pltpu.VMEM)] * count


def resident_call(name, body, operands, out_shape, scalars=(), after=()):
    taken = len(scalars) + len(operands)

    def kernel(*refs):
        body(*refs[:taken], *refs[taken + len(after) :])

    return pl.pallas_call(
        kernel,
        in_specs=[pl.BlockSpec(memory_space=pltpu.SMEM)] * len(scalars)
        + resident(len(operands))
        + [pl.BlockSpec(memory_space=pltpu.HBM)] * len(after),
        out_specs=resident(len(out_shape)),
        out_shape=out_shape,
        compiler_params=pltpu.CompilerParams(vmem_limit_bytes=VMEM_RESIDENT),
        name=name,
    )(*scalars, *operands, *after)


def wide(rows, columns):
    return pl.BlockSpec((rows, columns), lambda i, *_: (0, i))


def whole(rows, columns):
    return pl.BlockSpec((rows, columns), lambda i, *_: (0, 0))


def group(*shape):
    return pl.BlockSpec((1,) + shape, lambda i, *_: (i, 0, 0))


def local_states(keys, values, decays, groups, width, after=()):
    heads, tokens = decays.shape
    per, steps = heads // groups, groups // 2
    tall = per * (width + DECAY_ROWS)
    wider = wide(tokens, 2 * per * width)
    return local_call(
        "local_states",
        functools.partial(state_kernel, width),
        steps,
        (keys, values, decays),
        (wider, wider, whole(heads, tokens)),
        pl.BlockSpec((2, tall, width), lambda i: (i, 0, 0)),
        jax.ShapeDtypeStruct((groups, tall, width), BF16),
        scratch=(pltpu.VMEM((groups, tokens, per), F32), pltpu.VMEM((groups, 1, per), F32)),
        after=after,
    )


def local_intra(queries, keys, values, gate, within, across, width, after=()):
    tokens, groups, per = keys.shape[0], within.shape[0], within.shape[2]
    heads = wide(tokens, per * width)
    return local_call(
        "local_intra",
        functools.partial(intra_kernel, width),
        groups,
        (queries, keys, values, gate, within, across),
        (heads, heads, heads, heads, group(tokens, per), group(per, tokens)),
        [heads, heads],
        [jax.ShapeDtypeStruct(queries.shape, BF16)] * 2,
        after=after,
    )


def mix(queries, opened, intra, within, states, width, after=()):
    groups, tokens, per = within.shape
    heads = 2 * per
    wider = wide(tokens, heads * width)
    return local_call(
        "mix",
        functools.partial(mix_kernel, width),
        groups // 2,
        (queries, opened, intra, within, states),
        (
            wider,
            wider,
            wider,
            pl.BlockSpec((2, tokens, per), lambda i: (i, 0, 0)),
            pl.BlockSpec((heads, width, width), lambda i: (i, 0, 0)),
        ),
        [wide(tokens // 2, heads * width)] * 2,
        [jax.ShapeDtypeStruct((tokens // 2, queries.shape[1]), BF16)] * 2,
        after=after,
    )


def plane_total(parts, heads, width, after=()):
    shape = jax.ShapeDtypeStruct((heads, width + DECAY_ROWS, width), BF16)
    body = functools.partial(total_kernel, width)
    return resident_call("plane_total", body, (parts,), [shape], after=after)[0]


def join(earlier, later, width, after=()):
    shape = jax.ShapeDtypeStruct(later.shape, BF16)
    body = functools.partial(join_kernel, width)
    return resident_call("join", body, (earlier, later), [shape], after=after)[0]


def plane_prefix(parts, nearest, others, width, after=()):
    shape = jax.ShapeDtypeStruct((parts.shape[0], nearest.shape[0], width, width), BF16)
    body = functools.partial(prefix_kernel, width)
    return resident_call("plane_prefix", body, (parts, nearest, others), [shape], after=after)[0]


def deal_kernel(ways, block, place_ref, *refs):
    *source_refs, even_ref, odd_ref = refs
    for r in range(ways):
        target_ref, top = (even_ref, odd_ref)[r % 2], 0
        for source_ref in source_refs:
            rows = slice(top, top + source_ref.shape[0])
            for i in range(target_ref.shape[2] // block):
                start = pl.multiple_of((i * ways + (place_ref[0] ^ r)) * block, block)
                columns = slice(i * block, (i + 1) * block)
                target_ref[r // 2, rows, columns] = source_ref[:, pl.ds(start, block)]
            top += source_ref.shape[0]


def deal(arrays, place, ways, block, after=()):
    rows = sum(array.shape[0] for array in arrays)
    shape = jax.ShapeDtypeStruct((ways // 2, rows, arrays[0].shape[1] // ways), BF16)
    return resident_call(
        "deal",
        functools.partial(deal_kernel, ways, block),
        arrays,
        [shape, shape],
        scalars=(place.reshape(1),),
        after=after,
    )


def pair_kernel(parts, even_ref, odd_ref, *target_refs):
    for (chip, top), target_ref in zip(parts, target_refs):
        rows = slice(top, top + target_ref.shape[1])
        target_ref[0] = even_ref[chip, rows, :]
        target_ref[1] = odd_ref[chip, rows, :]


def pair(even, odd, split, after=()):
    chips, rows, columns = even.shape
    parts = [(chip, 0) for chip in range(chips)] + [(chips - 1, split)]
    heights = [rows] * (chips - 1) + [split, rows - split]
    return resident_call(
        "pair",
        functools.partial(pair_kernel, parts),
        (even, odd),
        [jax.ShapeDtypeStruct((2, height, columns), even.dtype) for height in heights],
        after=after,
    )


def order_kernel(place_ref, *refs):
    *sources, target_ref = refs
    rows = sources[-1].shape[1]
    for r in range(2 * len(sources)):
        source = sources[r // 2]
        start = pl.multiple_of((place_ref[0] ^ r) * rows, rows)
        target_ref[pl.ds(start, rows), :] = source[r % 2, source.shape[1] - rows :, :]


def in_order(arrays, place, after=()):
    _, rows, columns = arrays[-1].shape
    tall = (2 * len(arrays) * rows, columns)
    return resident_call(
        "in_order",
        order_kernel,
        arrays,
        [jax.ShapeDtypeStruct(tall, arrays[0].dtype)],
        scalars=(place.reshape(1),),
        after=after,
    )[0]


def hold(arrays, after):
    kept, count = pl.BlockSpec(memory_space=pltpu.HBM), len(arrays)
    return pl.pallas_call(
        lambda *refs: None,
        in_specs=[kept] * (count + len(after)),
        out_specs=[kept] * count,
        out_shape=[jax.ShapeDtypeStruct(array.shape, array.dtype) for array in arrays],
        input_output_aliases={i: i for i in range(count)},
        compiler_params=pltpu.CompilerParams(vmem_limit_bytes=VMEM_RESIDENT),
        name="hold",
    )(*arrays, *after)


def out_kernel(halves, *refs):
    chips, pieces = len(halves), 2 * len(halves)
    mixed, weight_ref, start_refs = refs[:pieces], refs[pieces], refs[pieces + 1 : -2]
    tokens, depth = mixed[0].shape
    step = min(depth, 512)
    total = jnp.zeros((pieces * tokens, weight_ref.shape[1]), F32)
    for start in range(0, depth, step):
        left = jnp.concatenate([ref[:, start : start + step] for ref in mixed], axis=0)
        total = total + dot(left, weight_ref[start : start + step, :], ((1,), (0,)))
    for chip in range(chips):
        rows = slice(halves[chip] * tokens, (halves[chip] + 1) * tokens)
        for core, out_ref in enumerate(refs[-2:]):
            i = 2 * chip + core
            hidden = start_refs[chip][core, rows, :].astype(F32)
            hidden = hidden + total[i * tokens : (i + 1) * tokens]
            out_ref[chip * tokens : (chip + 1) * tokens, :] = hidden.astype(BF16)


def out_projection(pieces, weight, after=()):
    halves, mixed, starts = zip(*pieces)
    mixed = [array for cores in mixed for array in cores]
    shape = jax.ShapeDtypeStruct((len(pieces) * mixed[0].shape[0], weight.shape[1]), BF16)
    return resident_call(
        "out_projection",
        functools.partial(out_kernel, halves),
        (*mixed, weight, *starts),
        [shape, shape],
        after=after,
    )


def cache_kernel(width, model, joined, finish, *refs):
    own_ref, other_ref, own_weight_ref, other_weight_ref, *refs = refs
    added, out_refs = refs[: len(joined)], refs[len(joined) :]
    tokens, columns = own_ref.shape[0] // 2, own_weight_ref.shape[1]
    own, other = own_ref[...], other_ref[...]
    total = dot(own, own_weight_ref[...], ((1,), (0,)))
    total = total + dot(other, other_weight_ref[...], ((1,), (0,)))
    squares = jnp.square(own.astype(F32)) + jnp.square(other.astype(F32))
    squares = jnp.sum(squares, axis=1, keepdims=True)
    for i in range(2):
        rows = slice(i * tokens, (i + 1) * tokens)
        sums, norm = total[rows], squares[rows]
        for ref, half in zip(added, joined):
            if half == i:
                sums = sums + ref[:, :columns].astype(F32)
                norm = norm + jnp.sum(ref[:, columns:].astype(F32), axis=1, keepdims=True)
        if finish:
            sums = (sums * lax.rsqrt(norm / model + NORM_EPS)).astype(BF16)
            for head in range(columns // (2 * width)):
                for kind, out_ref in enumerate(out_refs):
                    start = (2 * head + kind) * width
                    out_ref[rows, head * width : (head + 1) * width] = sums[:, start : start + width]
        else:
            high = norm.astype(BF16).astype(F32)
            middle = (norm - high).astype(BF16).astype(F32)
            low = norm - high - middle
            lane = lax.broadcasted_iota(jnp.int32, (tokens, width), 1)
            lanes = jnp.where(lane == 0, high, jnp.where(lane == 1, middle, 0.0))
            out_refs[i][:, :columns] = sums.astype(BF16)
            out_refs[i][:, columns:] = jnp.where(lane == 2, low, lanes).astype(BF16)


def cache_projection(own, other, weights, width, model, added=(), finish=False, after=()):
    tokens, columns = own.shape[0], weights[0].shape[1]
    out = (tokens, columns // 2) if finish else (tokens // 2, columns + width)
    return resident_call(
        "cache_projection",
        functools.partial(cache_kernel, width, model, [half for _, half in added], finish),
        (own, other, *weights, *[array for array, _ in added]),
        [jax.ShapeDtypeStruct(out, BF16)] * 2,
        after=after,
    )


SIZES = (4, 2, 2, 2)
DEVICES = math.prod(SIZES)
DEPTH = SIZES[0]
PLACES = DEVICES // DEPTH


def swap(array, distance):
    return lax.ppermute(array, SEQ, [(i, i ^ distance) for i in range(DEVICES)])


def hop(array, steps):
    pairs = [
        (a * PLACES + i, b * PLACES + i) for a, b in sorted(steps.items()) for i in range(PLACES)
    ]
    return lax.ppermute(array, SEQ, pairs)


def shared_on_device(
    queries, keys, values, gate, residual, log_decay, out_weight, norm_gain, kv_weight
):
    tokens, heads = log_decay.shape
    width = queries.shape[1] // heads
    model = out_weight.shape[1]
    share = model // PLACES
    piece = share // DEPTH
    core = lax.axis_index("c")
    place = 4 * lax.axis_index("y") + 2 * lax.axis_index("x") + core

    with jax.named_scope("kv_weight_gather"):
        kv_mine = lax.all_gather(kv_weight, "z", axis=0, tiled=True)
    running = jnp.cumsum(log_decay, axis=0)
    per = heads // PLACES
    within = running.reshape(tokens, PLACES, per).transpose(1, 0, 2)
    across = running.T.reshape(PLACES, per, tokens)
    states = local_states(keys, values, log_decay.T, PLACES, width)
    with jax.named_scope("state_scan"):
        parts = lax.all_to_all(states, PLANE, 0, 0, tiled=True)

    even, odd = deal((residual, out_weight), place, PLACES, piece, after=(states,))
    with jax.named_scope("start_exchange"):
        *starts, far_weight = pair(even, swap(odd, 1), tokens)
        starts[1:3] = [swap(starts[1], 2), swap(starts[2], 4)]
        far_weight = swap(far_weight, 6)
    with jax.named_scope("state_scan"):
        total = plane_total(parts, per, width, after=(starts[0],))
        nearest = hop(total, {a: a + 1 for a in range(DEPTH - 1)})
        joined = join(nearest, total, width)
        others = hop(joined, {a: a + 2 for a in range(DEPTH - 2)})
    with jax.named_scope("out_weight_gather"):
        shard = in_order((*starts[:3], far_weight), place, after=(total,))
        out_full = lax.all_gather(*hold((shard,), (kv_mine,)), "z", axis=0, tiled=True)
    with jax.named_scope("state_scan"):
        prefix = plane_prefix(
            parts, nearest, others, width, after=(kv_mine, shard)
        )
        entering = lax.all_to_all(prefix, PLANE, 0, 0, tiled=True)
        entering = entering.reshape(heads, width, width)
    intra, opened = local_intra(
        queries, keys, values, gate, within, across, width, after=(prefix,)
    )
    with jax.named_scope("residual_exchange"):
        (starts[3],) = hold((starts[3],), (joined,))
        starts[3] = swap(starts[3], 6)

    early, late = mix(queries, opened, intra, within, entering, width)
    early, late = hold((early, late), (starts[3],))

    with jax.named_scope("cache_weight"):
        gains = norm_gain.reshape(DEPTH, PLACES, piece)
        kv_full = []
        for r, rows in enumerate((kv_mine, swap(kv_mine, 1))):
            gain = lax.dynamic_index_in_dim(gains, place ^ r, 1, False).reshape(share, 1)
            kv_full.append((rows.astype(F32) * gain.astype(F32)).astype(BF16))

    def cores(mixed):
        return mixed, swap(mixed, 1)

    def hidden_of(*halves, after=()):
        pieces = [(half, mixed, starts[chip]) for chip, half, mixed in halves]
        mine, theirs = out_projection(pieces, out_full, after)
        return mine, swap(theirs, 1)

    def share_of(hidden, added=(), finish=False, after=()):
        return cache_projection(*hidden, kv_full, width, model, added, finish, after)

    with jax.named_scope("projections"):
        early_x, late_y = swap(early, 2), swap(late, 4)
        early_far, late_far = swap(early_x, 4), swap(late_y, 2)
        crossed = swap(early, 1), swap(late, 1)
        near = hidden_of(
            (1, 0, cores(early_x)), (2, 1, cores(late_y)), after=crossed
        )
        early, late = hold((early, late), (early_far, late_far))
        home = (0, 0, (early, crossed[0])), (0, 1, (late, crossed[1]))
        late_x, early_y = swap(late, 2), swap(early, 4)
        far = hidden_of((3, 0, cores(early_far)), (3, 1, cores(late_far)), after=(near[0],))
        early_far, late_far = share_of(far)
        early_x, late_y = share_of(near, after=(early_far,))
        late_x, early_y = hold((late_x, early_y), (early_x,))
        early_x, late_y = swap(early_x, 2), swap(late_y, 4)
        late_far, early_far = swap(late_far, 4), swap(early_far, 2)
        near = hidden_of((1, 1, cores(late_x)), (2, 0, cores(early_y)))
        late_x, early_y = share_of(near, [(late_far, 0), (early_far, 1)])
        home = hidden_of(*home, after=(late_x, early_x, late_y))
        late_x, early_y = swap(late_x, 2), swap(early_y, 4)
        added = [(early_x, 0), (late_x, 1), (early_y, 0), (late_y, 1)]
        return share_of(home, added, True)


def entering(part, axis, combine, identity):
    place = lax.axis_index(axis)
    gathered = jax.tree.map(lambda a: lax.all_gather(a, axis), part)
    state = jax.tree.map(lambda a, e: jnp.zeros_like(a) + jnp.asarray(e, a.dtype), part, identity)

    def one(step, state):
        return combine(
            state, jax.tree.map(lambda a: lax.dynamic_index_in_dim(a, step, 0, False), gathered)
        )

    return lax.fori_loop(0, place, one, state)


def local_retention(queries, keys, values, log_decay, block):
    tokens, heads, width = queries.shape
    count = tokens // block

    def to_blocks(array):
        return array.reshape((count, block) + array.shape[1:])

    lower = jnp.arange(block)[:, None] >= jnp.arange(block)[None, :]

    def advance(carry, inputs):
        state, offset = carry
        query_block, key_block, value_block, decay_block = inputs
        within = jnp.cumsum(decay_block, axis=0)
        spread = within[:, None, :] - within[None, :, :]
        factor = jnp.where(
            lower[:, :, None], jnp.exp(jnp.where(lower[:, :, None], spread, 0.0)), 0.0
        )
        scores = jnp.einsum(
            "ihd,jhd->hij", query_block, key_block, preferred_element_type=jnp.float32
        )
        weighted = scores * jnp.transpose(factor, (2, 0, 1))
        values_wide = value_block.astype(jnp.float32)
        intra = jnp.einsum("hij,jhd->ihd", weighted, values_wide, precision=HIGHEST)
        query_wide = query_block.astype(jnp.float32)
        carried = jnp.exp(within)[:, :, None] * jnp.einsum(
            "ihd,hde->ihe", query_wide, state, precision=HIGHEST
        )
        ending = within[-1]
        key_wide = key_block.astype(jnp.float32) * jnp.exp(ending[None, :] - within)[:, :, None]
        fresh = jnp.exp(ending)[:, None, None] * state + jnp.einsum(
            "jhd,jhe->hde", key_wide, values_wide, precision=HIGHEST
        )
        return ((fresh, offset + ending), (intra + carried, offset[None, :] + within))

    start = (jnp.zeros((heads, width, width), jnp.float32), jnp.zeros((heads,), jnp.float32))
    final, stacked = lax.scan(
        advance,
        start,
        (to_blocks(queries), to_blocks(keys), to_blocks(values), to_blocks(log_decay)),
    )
    return (
        stacked[0].reshape(tokens, heads, width),
        stacked[1].reshape(tokens, heads),
        final[0],
        final[1],
    )


def combine_states(earlier, later):
    return (earlier[0] * later[0], later[0][:, None, None] * earlier[1] + later[1])


def on_device(queries, keys, values, gate, residual, log_decay, out_weight, norm_gain, kv_weight):
    tokens = queries.shape[0]
    heads = log_decay.shape[1]
    width = queries.shape[1] // heads
    shaped = [array.reshape(tokens, heads, width) for array in (queries, keys, values)]
    partial_out, running, state, offset = local_retention(
        shaped[0], shaped[1], shaped[2], log_decay, min(512, tokens)
    )
    identity = (jnp.ones((heads,), jnp.float32), jnp.zeros((heads, width, width), jnp.float32))
    scan_decay, incoming = entering((jnp.exp(offset), state), "seq", combine_states, identity)
    retained = partial_out + jnp.exp(running)[:, :, None] * jnp.einsum(
        "thd,hde->the", shaped[0].astype(jnp.float32), incoming, precision=HIGHEST
    )
    scale = lax.rsqrt(jnp.mean(retained * retained, axis=2, keepdims=True) + 1e-06)
    mixed = (
        jax.nn.silu(gate.astype(jnp.float32)) * (retained * scale).reshape(tokens, heads * width)
    ).astype(jnp.bfloat16)
    all_heads = lax.all_gather(mixed, "head", axis=1, tiled=True)
    out_full, kv_full = (
        lax.all_gather(out_weight, "seq", axis=0, tiled=True),
        lax.all_gather(kv_weight, "seq", axis=0, tiled=True),
    )
    branch = jnp.dot(all_heads, out_full, preferred_element_type=jnp.float32)
    hidden = (residual.astype(jnp.float32) + branch).astype(jnp.bfloat16)
    wide = hidden.astype(jnp.float32)
    squares = lax.psum(jnp.sum(wide * wide, axis=1), "head")
    features = wide.shape[1] * lax.axis_size("head")
    inverse = lax.rsqrt(squares[:, None] / features + 1e-06)
    local_norm = (wide * inverse * norm_gain.astype(jnp.float32)[None, :]).astype(jnp.bfloat16)
    normalized = lax.all_gather(local_norm, "head", axis=1, tiled=True)
    projected = jnp.dot(normalized, kv_full, preferred_element_type=jnp.float32)
    cache_heads = kv_weight.shape[1] // (2 * width)
    arranged = projected.reshape(tokens, cache_heads, 2, width)
    cache_keys = arranged[:, :, 0, :].reshape(tokens, cache_heads * width).astype(jnp.bfloat16)
    cache_values = arranged[:, :, 1, :].reshape(tokens, cache_heads * width).astype(jnp.bfloat16)
    return (cache_keys, cache_values)


def solution(mesh):
    devices, split = mesh.shape["seq"], mesh.shape["head"]
    if split == 1 and devices == DEVICES:
        fine = Mesh(mesh.devices.reshape(SIZES + (1,)), SEQ + ("head",))
        placed, copied = P(SEQ, "head"), P("head")
        return jax.shard_map(
            shared_on_device,
            mesh=fine,
            in_specs=(placed,) * 7 + (copied, placed),
            out_specs=(placed, placed),
            check_vma=False,
        )
    placed = P("seq", "head")
    return jax.shard_map(
        on_device,
        mesh=mesh,
        in_specs=(placed,) * 7 + (P("head"), placed),
        out_specs=(placed, placed),
        check_vma=False,
    )
```

```python
import functools
import math

import jax
import jax.numpy as jnp
from jax import lax
from jax.experimental import pallas as pl
from jax.experimental.pallas import tpu as pltpu
from jax.sharding import Mesh
from jax.sharding import PartitionSpec as P

F32, BF16 = jnp.float32, jnp.bfloat16
HIGHEST = lax.Precision.HIGHEST
NORM_EPS = 1e-06
DECAY_ROWS = 16
PLANE = ("y", "x", "c")
SEQ = ("z", "y", "x", "c")
MIB = 1024 * 1024
VMEM_STREAMED = {"local_states": 60 * MIB, "local_intra": 54 * MIB, "mix": 60 * MIB}
VMEM_RESIDENT = 16 * MIB


def split_rows(total):
    high = total.astype(BF16).astype(F32)
    middle = (total - high).astype(BF16).astype(F32)
    low = total - high - middle
    row = lax.broadcasted_iota(jnp.int32, (DECAY_ROWS, total.shape[1]), 0)
    rows = jnp.where(row == 0, high, jnp.where(row == 1, middle, jnp.where(row == 2, low, 0.0)))
    return rows.astype(BF16)


def join_rows(rows):
    return jnp.sum(rows.astype(F32), axis=0, keepdims=True)


def dot(a, b, contract):
    return lax.dot_general(a, b, (contract, ((), ())), preferred_element_type=F32)


def state_kernel(width, key_ref, value_ref, decay_ref, out_ref, fade_ref, ending_ref):
    tokens = key_ref.shape[0]
    groups, _, per = fade_ref.shape

    @pl.when(pl.program_id(0) == 0)
    def _():
        decay = decay_ref[...]
        later = lax.broadcasted_iota(jnp.int32, (tokens, tokens), 0) < lax.broadcasted_iota(
            jnp.int32, (tokens, tokens), 1
        )
        rest = lax.dot_general(
            later.astype(F32),
            decay,
            (((1,), (1,)), ((), ())),
            precision=HIGHEST,
            preferred_element_type=F32,
        )
        fade = jnp.exp(rest)
        ending = rest[:1] + jnp.transpose(decay)[:1]
        for i in range(groups):
            fade_ref[i] = fade[:, i * per : (i + 1) * per]
            ending_ref[i] = ending[:, i * per : (i + 1) * per]

    rows = width + DECAY_ROWS
    for i in range(out_ref.shape[0]):
        place = pl.program_id(0) * out_ref.shape[0] + i
        fade, ending = fade_ref[place], ending_ref[place]
        for head in range(per):
            columns = slice((i * per + head) * width, (i * per + head + 1) * width)
            faded = (key_ref[:, columns].astype(F32) * fade[:, head : head + 1]).astype(BF16)
            state = dot(faded, value_ref[:, columns], ((0,), (0,)))
            out_ref[i, head * rows : head * rows + width, :] = state.astype(BF16)
            total = jnp.broadcast_to(ending[:, head : head + 1], (1, width))
            out_ref[i, head * rows + width : (head + 1) * rows, :] = split_rows(total)


def intra_kernel(
    width, query_ref, key_ref, value_ref, gate_ref, within_ref, across_ref, out_ref, open_ref
):
    tokens = query_ref.shape[0]
    within, across = within_ref[0], across_ref[0]
    lower = lax.broadcasted_iota(jnp.int32, (tokens, tokens), 0) >= lax.broadcasted_iota(
        jnp.int32, (tokens, tokens), 1
    )
    for head in range(within.shape[1]):
        columns = slice(head * width, (head + 1) * width)
        scores = dot(query_ref[:, columns], key_ref[:, columns], ((1,), (1,)))
        spread = within[:, head : head + 1] - across[head : head + 1, :]
        weighted = jnp.where(lower, scores * jnp.exp(jnp.where(lower, spread, 0.0)), 0.0)
        local = dot(weighted.astype(BF16), value_ref[:, columns], ((1,), (0,)))
        out_ref[:, columns] = local.astype(BF16)
        gate = gate_ref[:, columns].astype(F32)
        open_ref[:, columns] = (gate / (1.0 + jnp.exp(-gate))).astype(BF16)


def mix_kernel(width, query_ref, open_ref, intra_ref, within_ref, state_ref, *out_refs):
    rows = out_refs[0].shape[0]
    groups, _, per = within_ref.shape
    for head in range(groups * per):
        reach = jnp.exp(within_ref[head // per])[:, head % per : head % per + 1]
        columns = slice(head * width, (head + 1) * width)
        carried = dot(query_ref[:, columns], state_ref[head], ((1,), (0,)))
        retained = intra_ref[:, columns].astype(F32) + reach * carried
        scale = lax.rsqrt(jnp.mean(retained * retained, axis=1, keepdims=True) + NORM_EPS)
        mixed = (open_ref[:, columns].astype(F32) * (retained * scale)).astype(BF16)
        for half, out_ref in enumerate(out_refs):
            out_ref[:, columns] = mixed[half * rows : (half + 1) * rows]


def total_kernel(width, parts_ref, out_ref):
    for head in range(out_ref.shape[0]):
        top = head * (width + DECAY_ROWS)
        states, decays = slice(top, top + width), slice(top + width, top + width + DECAY_ROWS)
        state = jnp.zeros((width, width), F32)
        total = jnp.zeros((1, width), F32)
        for place in range(parts_ref.shape[0]):
            ending = join_rows(parts_ref[place, decays, :])
            state = jnp.exp(ending) * state + parts_ref[place, states, :].astype(F32)
            total = total + ending
        out_ref[head, :width, :] = state.astype(BF16)
        out_ref[head, width:, :] = split_rows(total)


def join_kernel(width, earlier_ref, later_ref, out_ref):
    for head in range(out_ref.shape[0]):
        ending = join_rows(later_ref[head, width:, :])
        state = jnp.exp(ending) * earlier_ref[head, :width, :].astype(F32)
        out_ref[head, :width, :] = (state + later_ref[head, :width, :].astype(F32)).astype(BF16)
        out_ref[head, width:, :] = split_rows(join_rows(earlier_ref[head, width:, :]) + ending)


def prefix_kernel(width, parts_ref, nearest_ref, others_ref, out_ref):
    for head in range(nearest_ref.shape[0]):
        top = head * (width + DECAY_ROWS)
        states, decays = slice(top, top + width), slice(top + width, top + width + DECAY_ROWS)
        reach = jnp.exp(join_rows(nearest_ref[head, width:, :]))
        state = reach * others_ref[head, :width, :].astype(F32)
        state = state + nearest_ref[head, :width, :].astype(F32)
        for place in range(parts_ref.shape[0]):
            out_ref[place, head] = state.astype(BF16)
            ending = join_rows(parts_ref[place, decays, :])
            state = jnp.exp(ending) * state + parts_ref[place, states, :].astype(F32)


def local_call(
    name, body, grid, operands, specs, out_specs, out_shape, scalars=(), scratch=(), after=()
):
    taken = len(scalars) + len(operands)

    def kernel(*refs):
        body(*refs[:taken], *refs[taken + len(after) :])

    return pl.pallas_call(
        kernel,
        grid_spec=pltpu.PrefetchScalarGridSpec(
            num_scalar_prefetch=len(scalars),
            grid=(grid,),
            in_specs=list(specs) + [pl.BlockSpec(memory_space=pltpu.HBM)] * len(after),
            out_specs=out_specs,
            scratch_shapes=scratch,
        ),
        out_shape=out_shape,
        compiler_params=pltpu.CompilerParams(vmem_limit_bytes=VMEM_STREAMED[name]),
        name=name,
    )(*scalars, *operands, *after)


def resident(count):
    return [pl.BlockSpec(memory_space=pltpu.VMEM)] * count


def resident_call(name, body, operands, out_shape, scalars=(), after=()):
    taken = len(scalars) + len(operands)

    def kernel(*refs):
        body(*refs[:taken], *refs[taken + len(after) :])

    return pl.pallas_call(
        kernel,
        in_specs=[pl.BlockSpec(memory_space=pltpu.SMEM)] * len(scalars)
        + resident(len(operands))
        + [pl.BlockSpec(memory_space=pltpu.HBM)] * len(after),
        out_specs=resident(len(out_shape)),
        out_shape=out_shape,
        compiler_params=pltpu.CompilerParams(vmem_limit_bytes=VMEM_RESIDENT),
        name=name,
    )(*scalars, *operands, *after)


def wide(rows, columns):
    return pl.BlockSpec((rows, columns), lambda i, *_: (0, i))


def whole(rows, columns):
    return pl.BlockSpec((rows, columns), lambda i, *_: (0, 0))


def group(*shape):
    return pl.BlockSpec((1,) + shape, lambda i, *_: (i, 0, 0))


def local_states(keys, values, decays, groups, width, after=()):
    heads, tokens = decays.shape
    per, steps = heads // groups, groups // 2
    tall = per * (width + DECAY_ROWS)
    wider = wide(tokens, 2 * per * width)
    return local_call(
        "local_states",
        functools.partial(state_kernel, width),
        steps,
        (keys, values, decays),
        (wider, wider, whole(heads, tokens)),
        pl.BlockSpec((2, tall, width), lambda i: (i, 0, 0)),
        jax.ShapeDtypeStruct((groups, tall, width), BF16),
        scratch=(pltpu.VMEM((groups, tokens, per), F32), pltpu.VMEM((groups, 1, per), F32)),
        after=after,
    )


def local_intra(queries, keys, values, gate, within, across, width, after=()):
    tokens, groups, per = keys.shape[0], within.shape[0], within.shape[2]
    heads = wide(tokens, per * width)
    return local_call(
        "local_intra",
        functools.partial(intra_kernel, width),
        groups,
        (queries, keys, values, gate, within, across),
        (heads, heads, heads, heads, group(tokens, per), group(per, tokens)),
        [heads, heads],
        [jax.ShapeDtypeStruct(queries.shape, BF16)] * 2,
        after=after,
    )


def mix(queries, opened, intra, within, states, width, after=()):
    groups, tokens, per = within.shape
    heads = 2 * per
    wider = wide(tokens, heads * width)
    return local_call(
        "mix",
        functools.partial(mix_kernel, width),
        groups // 2,
        (queries, opened, intra, within, states),
        (
            wider,
            wider,
            wider,
            pl.BlockSpec((2, tokens, per), lambda i: (i, 0, 0)),
            pl.BlockSpec((heads, width, width), lambda i: (i, 0, 0)),
        ),
        [wide(tokens // 2, heads * width)] * 2,
        [jax.ShapeDtypeStruct((tokens // 2, queries.shape[1]), BF16)] * 2,
        after=after,
    )


def plane_total(parts, heads, width, after=()):
    shape = jax.ShapeDtypeStruct((heads, width + DECAY_ROWS, width), BF16)
    body = functools.partial(total_kernel, width)
    return resident_call("plane_total", body, (parts,), [shape], after=after)[0]


def join(earlier, later, width, after=()):
    shape = jax.ShapeDtypeStruct(later.shape, BF16)
    body = functools.partial(join_kernel, width)
    return resident_call("join", body, (earlier, later), [shape], after=after)[0]


def plane_prefix(parts, nearest, others, width, after=()):
    shape = jax.ShapeDtypeStruct((parts.shape[0], nearest.shape[0], width, width), BF16)
    body = functools.partial(prefix_kernel, width)
    return resident_call("plane_prefix", body, (parts, nearest, others), [shape], after=after)[0]


def dealt_blocks(ways, block, source_refs, place):
    top = 0
    for source_ref in source_refs:
        rows = source_ref.shape[0]
        for i in range(source_ref.shape[1] // (ways * block)):
            start = pl.multiple_of((i * ways + place) * block, block)
            yield slice(top, top + rows), slice(i * block, (i + 1) * block), source_ref[:, pl.ds(start, block)]
        top += rows


def deal_kernel(ways, block, place_ref, *refs):
    *source_refs, target_ref = refs
    for r in range(1, ways, 2):
        for rows, columns, part in dealt_blocks(ways, block, source_refs, place_ref[0] ^ r):
            target_ref[r // 2, rows, columns] = part


def deal(arrays, place, ways, block, after=()):
    rows = sum(array.shape[0] for array in arrays)
    shape = jax.ShapeDtypeStruct((ways // 2, rows, arrays[0].shape[1] // ways), BF16)
    return resident_call(
        "deal",
        functools.partial(deal_kernel, ways, block),
        arrays,
        [shape],
        scalars=(place.reshape(1),),
        after=after,
    )[0]


def pair_kernel(ways, block, split, place_ref, *refs):
    chips, sources = ways // 2, len(refs) - ways // 2 - 2
    source_refs, odd_ref, target_refs = refs[:sources], refs[sources], refs[sources + 1 :]
    for chip in range(chips):
        for rows, columns, part in dealt_blocks(ways, block, source_refs, place_ref[0] ^ (2 * chip)):
            target_ref = target_refs[chip]
            if rows.start >= target_ref.shape[1]:
                target_ref, rows = target_refs[chips], slice(rows.start - split, rows.stop - split)
            target_ref[0, rows, columns] = part
        height = target_refs[chip].shape[1]
        target_refs[chip][1] = odd_ref[chip, :height, :]
    target_refs[chips][1] = odd_ref[chips - 1, split:, :]


def pair(arrays, odd, place, ways, block, after=()):
    chips, rows, columns = odd.shape
    split = rows - arrays[-1].shape[0]
    heights = [rows] * (chips - 1) + [split, rows - split]
    return resident_call(
        "pair",
        functools.partial(pair_kernel, ways, block, split),
        (*arrays, odd),
        [jax.ShapeDtypeStruct((2, height, columns), odd.dtype) for height in heights],
        scalars=(place.reshape(1),),
        after=after,
    )


def order_kernel(place_ref, *refs):
    *sources, target_ref = refs
    rows = sources[-1].shape[1]
    for r in range(2 * len(sources)):
        source = sources[r // 2]
        start = pl.multiple_of((place_ref[0] ^ r) * rows, rows)
        target_ref[pl.ds(start, rows), :] = source[r % 2, source.shape[1] - rows :, :]


def in_order(arrays, place, after=()):
    _, rows, columns = arrays[-1].shape
    tall = (2 * len(arrays) * rows, columns)
    return resident_call(
        "in_order",
        order_kernel,
        arrays,
        [jax.ShapeDtypeStruct(tall, arrays[0].dtype)],
        scalars=(place.reshape(1),),
        after=after,
    )[0]


def hold(arrays, after):
    kept, count = pl.BlockSpec(memory_space=pltpu.HBM), len(arrays)
    return pl.pallas_call(
        lambda *refs: None,
        in_specs=[kept] * (count + len(after)),
        out_specs=[kept] * count,
        out_shape=[jax.ShapeDtypeStruct(array.shape, array.dtype) for array in arrays],
        input_output_aliases={i: i for i in range(count)},
        compiler_params=pltpu.CompilerParams(vmem_limit_bytes=VMEM_RESIDENT),
        name="hold",
    )(*arrays, *after)


def out_kernel(halves, *refs):
    chips, pieces = len(halves), 2 * len(halves)
    mixed, weight_ref, start_refs = refs[:pieces], refs[pieces], refs[pieces + 1 : -2]
    tokens, depth = mixed[0].shape
    step = min(depth, 512)
    total = jnp.zeros((pieces * tokens, weight_ref.shape[1]), F32)
    for start in range(0, depth, step):
        left = jnp.concatenate([ref[:, start : start + step] for ref in mixed], axis=0)
        total = total + dot(left, weight_ref[start : start + step, :], ((1,), (0,)))
    for chip in range(chips):
        rows = slice(halves[chip] * tokens, (halves[chip] + 1) * tokens)
        for core, out_ref in enumerate(refs[-2:]):
            i = 2 * chip + core
            hidden = start_refs[chip][core, rows, :].astype(F32)
            hidden = hidden + total[i * tokens : (i + 1) * tokens]
            out_ref[chip * tokens : (chip + 1) * tokens, :] = hidden.astype(BF16)


def out_projection(pieces, weight, after=()):
    halves, mixed, starts = zip(*pieces)
    mixed = [array for cores in mixed for array in cores]
    shape = jax.ShapeDtypeStruct((len(pieces) * mixed[0].shape[0], weight.shape[1]), BF16)
    return resident_call(
        "out_projection",
        functools.partial(out_kernel, halves),
        (*mixed, weight, *starts),
        [shape, shape],
        after=after,
    )


def cache_kernel(width, joined, *refs):
    own_ref, other_ref, own_weight_ref, other_weight_ref, *refs = refs
    added, out_refs = refs[: len(joined)], refs[len(joined) :]
    tokens, columns = own_ref.shape[0] // 2, own_weight_ref.shape[1]
    own, other = own_ref[...], other_ref[...]
    total = dot(own, own_weight_ref[...], ((1,), (0,)))
    total = total + dot(other, other_weight_ref[...], ((1,), (0,)))
    squares = jnp.square(own.astype(F32)) + jnp.square(other.astype(F32))
    squares = jnp.sum(squares, axis=1, keepdims=True)
    for i in range(2):
        rows = slice(i * tokens, (i + 1) * tokens)
        sums, norm = total[rows], squares[rows]
        for ref, half in zip(added, joined):
            if half == i:
                sums = sums + ref[:, :columns].astype(F32)
                norm = norm + jnp.sum(ref[:, columns:].astype(F32), axis=1, keepdims=True)
        high = norm.astype(BF16).astype(F32)
        middle = (norm - high).astype(BF16).astype(F32)
        low = norm - high - middle
        lane = lax.broadcasted_iota(jnp.int32, (tokens, width), 1)
        lanes = jnp.where(lane == 0, high, jnp.where(lane == 1, middle, 0.0))
        out_refs[i][:, :columns] = sums.astype(BF16)
        out_refs[i][:, columns:] = jnp.where(lane == 2, low, lanes).astype(BF16)


def finish_kernel(width, model, *refs):
    *share_refs, keys_ref, values_ref = refs
    tokens, columns = share_refs[0].shape[0], 2 * keys_ref.shape[1]
    for half in range(2):
        shares = [ref[...].astype(F32) for ref in share_refs[half::2]]
        norm = sum(jnp.sum(share[:, columns:], axis=1, keepdims=True) for share in shares)
        sums = sum(share[:, :columns] for share in shares)
        sums = (sums * lax.rsqrt(norm / model + NORM_EPS)).astype(BF16)
        rows = slice(half * tokens, (half + 1) * tokens)
        for head in range(columns // (2 * width)):
            for kind, out_ref in enumerate((keys_ref, values_ref)):
                start = (2 * head + kind) * width
                out_ref[rows, head * width : (head + 1) * width] = sums[:, start : start + width]


def finish(shares, width, model):
    tokens, columns = shares[0].shape
    out = jax.ShapeDtypeStruct((2 * tokens, (columns - width) // 2), BF16)
    body = functools.partial(finish_kernel, width, model)
    return resident_call("finish", body, shares, [out, out])


def cache_projection(own, other, weights, width, joined=(), added=(), after=()):
    tokens, columns = own.shape[0], weights[0].shape[1]
    out = jax.ShapeDtypeStruct((tokens // 2, columns + width), BF16)
    return resident_call(
        "cache_projection",
        functools.partial(cache_kernel, width, joined),
        (own, other, *weights, *added),
        [out, out],
        after=after,
    )


SIZES = (4, 2, 2, 2)
DEVICES = math.prod(SIZES)
DEPTH = SIZES[0]
PLACES = DEVICES // DEPTH


def swap(array, distance):
    return lax.ppermute(array, SEQ, [(i, i ^ distance) for i in range(DEVICES)])


def hop(array, steps):
    pairs = [
        (a * PLACES + i, b * PLACES + i) for a, b in sorted(steps.items()) for i in range(PLACES)
    ]
    return lax.ppermute(array, SEQ, pairs)


def shared_on_device(
    queries, keys, values, gate, residual, log_decay, out_weight, norm_gain, kv_weight
):
    tokens, heads = log_decay.shape
    width = queries.shape[1] // heads
    model = out_weight.shape[1]
    share = model // PLACES
    piece = share // DEPTH
    core = lax.axis_index("c")
    place = 4 * lax.axis_index("y") + 2 * lax.axis_index("x") + core

    with jax.named_scope("kv_weight_gather"):
        kv_mine = lax.all_gather(kv_weight, "z", axis=0, tiled=True)
    running = jnp.cumsum(log_decay, axis=0)
    per = heads // PLACES
    within = running.reshape(tokens, PLACES, per).transpose(1, 0, 2)
    across = running.T.reshape(PLACES, per, tokens)
    states = local_states(keys, values, log_decay.T, PLACES, width)
    with jax.named_scope("state_scan"):
        parts = lax.all_to_all(states, PLANE, 0, 0, tiled=True)

    dealt = (residual, out_weight)
    odd = deal(dealt, place, PLACES, piece, after=(states,))
    with jax.named_scope("start_exchange"):
        *starts, far_weight = pair(dealt, swap(odd, 1), place, PLACES, piece)
        starts[1:3] = [swap(starts[1], 2), swap(starts[2], 4)]
        far_weight = swap(far_weight, 6)
    with jax.named_scope("state_scan"):
        total = plane_total(parts, per, width, after=(starts[0],))
        nearest = hop(total, {a: a + 1 for a in range(DEPTH - 1)})
        joined = join(nearest, total, width)
        others = hop(joined, {a: a + 2 for a in range(DEPTH - 2)})
    with jax.named_scope("out_weight_gather"):
        shard = in_order((*starts[:3], far_weight), place, after=(total,))
        out_full = lax.all_gather(*hold((shard,), (kv_mine,)), "z", axis=0, tiled=True)
    with jax.named_scope("state_scan"):
        prefix = plane_prefix(
            parts, nearest, others, width, after=(kv_mine, shard)
        )
        entering = lax.all_to_all(prefix, PLANE, 0, 0, tiled=True)
        entering = entering.reshape(heads, width, width)
    intra, opened = local_intra(
        queries, keys, values, gate, within, across, width, after=(prefix,)
    )
    with jax.named_scope("residual_exchange"):
        (starts[3],) = hold((starts[3],), (joined,))
        starts[3] = swap(starts[3], 6)

    early, late = mix(queries, opened, intra, within, entering, width)
    early, late = hold((early, late), (starts[3],))

    with jax.named_scope("cache_weight"):
        gains = norm_gain.reshape(DEPTH, PLACES, piece)
        kv_full = []
        for r, rows in enumerate((kv_mine, swap(kv_mine, 1))):
            gain = lax.dynamic_index_in_dim(gains, place ^ r, 1, False).reshape(share, 1)
            kv_full.append((rows.astype(F32) * gain.astype(F32)).astype(BF16))

    def cores(mixed):
        return mixed, swap(mixed, 1)

    def hidden_of(*halves, after=()):
        pieces = [(half, mixed, starts[chip]) for chip, half, mixed in halves]
        mine, theirs = out_projection(pieces, out_full, after)
        return mine, swap(theirs, 1)

    def share_of(hidden, joined=(), added=(), after=()):
        return cache_projection(*hidden, kv_full, width, joined, added, after)

    with jax.named_scope("projections"):
        early_x, late_y = swap(early, 2), swap(late, 4)
        early_far, late_far = swap(early_x, 4), swap(late_y, 2)
        crossed = swap(early, 1), swap(late, 1)
        near = hidden_of(
            (1, 0, cores(early_x)), (2, 1, cores(late_y)), after=crossed
        )
        early, late = hold((early, late), (early_far, late_far))
        home = (0, 0, (early, crossed[0])), (0, 1, (late, crossed[1]))
        late_x, early_y = swap(late, 2), swap(early, 4)
        far = hidden_of((3, 0, cores(early_far)), (3, 1, cores(late_far)), after=(near[0],))
        early_far, late_far = share_of(far)
        early_x, late_y = share_of(near, after=(early_far,))
        late_x, early_y = hold((late_x, early_y), (early_x,))
        early_x, late_y = swap(early_x, 2), swap(late_y, 4)
        late_far, early_far = swap(late_far, 4), swap(early_far, 2)
        near = hidden_of((1, 1, cores(late_x)), (2, 0, cores(early_y)))
        late_x, early_y = share_of(near, (0, 1), (late_far, early_far))
        home = hidden_of(*home, after=(late_x, early_x, late_y))
        late_x, early_y = swap(late_x, 2), swap(early_y, 4)
        home = share_of(home, (0, 1), (early_x, late_y))
        return finish((*home, early_y, late_x), width, model)


def entering(part, axis, combine, identity):
    place = lax.axis_index(axis)
    gathered = jax.tree.map(lambda a: lax.all_gather(a, axis), part)
    state = jax.tree.map(lambda a, e: jnp.zeros_like(a) + jnp.asarray(e, a.dtype), part, identity)

    def one(step, state):
        return combine(
            state, jax.tree.map(lambda a: lax.dynamic_index_in_dim(a, step, 0, False), gathered)
        )

    return lax.fori_loop(0, place, one, state)


def local_retention(queries, keys, values, log_decay, block):
    tokens, heads, width = queries.shape
    count = tokens // block

    def to_blocks(array):
        return array.reshape((count, block) + array.shape[1:])

    lower = jnp.arange(block)[:, None] >= jnp.arange(block)[None, :]

    def advance(carry, inputs):
        state, offset = carry
        query_block, key_block, value_block, decay_block = inputs
        within = jnp.cumsum(decay_block, axis=0)
        spread = within[:, None, :] - within[None, :, :]
        factor = jnp.where(
            lower[:, :, None], jnp.exp(jnp.where(lower[:, :, None], spread, 0.0)), 0.0
        )
        scores = jnp.einsum(
            "ihd,jhd->hij", query_block, key_block, preferred_element_type=jnp.float32
        )
        weighted = scores * jnp.transpose(factor, (2, 0, 1))
        values_wide = value_block.astype(jnp.float32)
        intra = jnp.einsum("hij,jhd->ihd", weighted, values_wide, precision=HIGHEST)
        query_wide = query_block.astype(jnp.float32)
        carried = jnp.exp(within)[:, :, None] * jnp.einsum(
            "ihd,hde->ihe", query_wide, state, precision=HIGHEST
        )
        ending = within[-1]
        key_wide = key_block.astype(jnp.float32) * jnp.exp(ending[None, :] - within)[:, :, None]
        fresh = jnp.exp(ending)[:, None, None] * state + jnp.einsum(
            "jhd,jhe->hde", key_wide, values_wide, precision=HIGHEST
        )
        return ((fresh, offset + ending), (intra + carried, offset[None, :] + within))

    start = (jnp.zeros((heads, width, width), jnp.float32), jnp.zeros((heads,), jnp.float32))
    final, stacked = lax.scan(
        advance,
        start,
        (to_blocks(queries), to_blocks(keys), to_blocks(values), to_blocks(log_decay)),
    )
    return (
        stacked[0].reshape(tokens, heads, width),
        stacked[1].reshape(tokens, heads),
        final[0],
        final[1],
    )


def combine_states(earlier, later):
    return (earlier[0] * later[0], later[0][:, None, None] * earlier[1] + later[1])


def on_device(queries, keys, values, gate, residual, log_decay, out_weight, norm_gain, kv_weight):
    tokens = queries.shape[0]
    heads = log_decay.shape[1]
    width = queries.shape[1] // heads
    shaped = [array.reshape(tokens, heads, width) for array in (queries, keys, values)]
    partial_out, running, state, offset = local_retention(
        shaped[0], shaped[1], shaped[2], log_decay, min(512, tokens)
    )
    identity = (jnp.ones((heads,), jnp.float32), jnp.zeros((heads, width, width), jnp.float32))
    scan_decay, incoming = entering((jnp.exp(offset), state), "seq", combine_states, identity)
    retained = partial_out + jnp.exp(running)[:, :, None] * jnp.einsum(
        "thd,hde->the", shaped[0].astype(jnp.float32), incoming, precision=HIGHEST
    )
    scale = lax.rsqrt(jnp.mean(retained * retained, axis=2, keepdims=True) + 1e-06)
    mixed = (
        jax.nn.silu(gate.astype(jnp.float32)) * (retained * scale).reshape(tokens, heads * width)
    ).astype(jnp.bfloat16)
    all_heads = lax.all_gather(mixed, "head", axis=1, tiled=True)
    out_full, kv_full = (
        lax.all_gather(out_weight, "seq", axis=0, tiled=True),
        lax.all_gather(kv_weight, "seq", axis=0, tiled=True),
    )
    branch = jnp.dot(all_heads, out_full, preferred_element_type=jnp.float32)
    hidden = (residual.astype(jnp.float32) + branch).astype(jnp.bfloat16)
    wide = hidden.astype(jnp.float32)
    squares = lax.psum(jnp.sum(wide * wide, axis=1), "head")
    features = wide.shape[1] * lax.axis_size("head")
    inverse = lax.rsqrt(squares[:, None] / features + 1e-06)
    local_norm = (wide * inverse * norm_gain.astype(jnp.float32)[None, :]).astype(jnp.bfloat16)
    normalized = lax.all_gather(local_norm, "head", axis=1, tiled=True)
    projected = jnp.dot(normalized, kv_full, preferred_element_type=jnp.float32)
    cache_heads = kv_weight.shape[1] // (2 * width)
    arranged = projected.reshape(tokens, cache_heads, 2, width)
    cache_keys = arranged[:, :, 0, :].reshape(tokens, cache_heads * width).astype(jnp.bfloat16)
    cache_values = arranged[:, :, 1, :].reshape(tokens, cache_heads * width).astype(jnp.bfloat16)
    return (cache_keys, cache_values)


def solution(mesh):
    devices, split = mesh.shape["seq"], mesh.shape["head"]
    if split == 1 and devices == DEVICES:
        fine = Mesh(mesh.devices.reshape(SIZES + (1,)), SEQ + ("head",))
        placed, copied = P(SEQ, "head"), P("head")
        return jax.shard_map(
            shared_on_device,
            mesh=fine,
            in_specs=(placed,) * 7 + (copied, placed),
            out_specs=(placed, placed),
            check_vma=False,
        )
    placed = P("seq", "head")
    return jax.shard_map(
        on_device,
        mesh=mesh,
        in_specs=(placed,) * 7 + (P("head"), placed),
        out_specs=(placed, placed),
        check_vma=False,
    )
```
